768 devices in a mesh: space: 192 (over y_lo, z, x, core), tm: 4 (over y_hi).
Axes of the slice: x: 4, y: 8 (y_hi: 4, y_lo: 2; y = y_hi * 2 + y_lo), z: 12, core: 2. Of those that a mesh axis runs over, the one named last changes fastest.
Arguments:
- guess_pressure: float32 [4, 384, 64, 128], P('tm', 'space'), may hold values from -6 to 6
- guess_velocity: float32 [4, 3, 384, 64, 128], P('tm', None, 'space'), may hold values from -6 to 6
- initial_pressure: float32 [384, 64, 128], P('space'), may hold values from -6 to 6
- initial_velocity: float32 [3, 384, 64, 128], P(None, 'space'), may hold values from -6 to 6
- stiffness: float32 [384, 64, 128], P('space'), may hold values from 0.5 to 2
- inv_mass: float32 [384, 64, 128], P('space'), may hold values from 0.5 to 2
Outputs:
- corrected_pressure: float32 [4, 384, 64, 128], P('tm', 'space')
- corrected_velocity: float32 [4, 3, 384, 64, 128], P('tm', None, 'space')
- residual_pressure: float32 [4, 384, 64, 128], P('tm', 'space')
- residual_velocity: float32 [4, 3, 384, 64, 128], P('tm', None, 'space')
The draws below stay inside these ranges and needn't reach their ends.
All inputs are finite; a program needn't handle non-finite values.
Results may differ from the reference program's by a relative error of at most 0.00002.
Values sent between devices are 32-bit elements; how exact they have to be, the bound alone decides.
A program may use at most 32 MiB of HBM per device.

```python
import math
import jax
import jax.numpy as jnp

NY = 64
NZ = 128
STEPS = 4
NX = 384
N_TM = 4


def steps_of(stream_key, dims, pieces, least, top_value):
    loudness, own = 1.0, jax.random.fold_in(stream_key, 6)
    for position, blocks in pieces:
        heights = jnp.exp(jax.random.uniform(jax.random.fold_in(own, position), (blocks,), jnp.float32, least / len(pieces), top_value / len(pieces)))
        loudness = loudness * jnp.repeat(heights, dims[position] // blocks).reshape([-1 if axis == position else 1 for axis in range(len(dims))])
    return loudness


def bell_draw(stream_key, dims, deviation, limit, cuts=(), dtype=jnp.bfloat16):
    factor_of = steps_of(stream_key, dims, cuts, -0.22, 0.18) if cuts else 1.0
    values = jax.random.normal(stream_key, dims, jnp.float32) * deviation * factor_of
    return jnp.minimum(jnp.maximum(values, -limit), limit).astype(dtype)


def setup_inputs(seed: int = 0) -> dict:
    splits = jax.random.split(jax.random.key(seed), 7)
    return {
        "guess_pressure": bell_draw(splits[0], (N_TM, NX, NY, NZ), 1.0, 6.0, ((0, 4), (1, 192)), jnp.float32),
        "guess_velocity": bell_draw(splits[1], (N_TM, 3, NX, NY, NZ), 1.0, 6.0, ((0, 4), (2, 192)), jnp.float32),
        "initial_pressure": bell_draw(splits[2], (NX, NY, NZ), 1.0, 6.0, ((0, 192),), jnp.float32),
        "initial_velocity": bell_draw(splits[3], (3, NX, NY, NZ), 1.0, 6.0, ((1, 192),), jnp.float32),
        "stiffness": jnp.clip(jnp.exp(math.log(2.0) - 1.3862944 * jax.random.uniform(splits[4], (NX, NY, NZ), jnp.float32) ** steps_of(splits[4], (NX, NY, NZ), ((0, 192),), -0.2, 0.2)), 0.5, 2.0),
        "inv_mass": jnp.clip(jnp.exp(math.log(2.0) - 1.3862944 * jax.random.uniform(splits[5], (NX, NY, NZ), jnp.float32) ** steps_of(splits[5], (NX, NY, NZ), ((0, 192),), -0.2, 0.2)), 0.5, 2.0),
    }


DT_COARSE = 0.4


def neighbour_sum(values, offset, axis):
    return values + jnp.roll(values, offset, axis=axis)


def node_forces(pressure, lower_zones):
    combined = pressure + lower_zones
    force_x = 0.25 * (neighbour_sum(neighbour_sum(lower_zones, 1, -1), 1, -2) - neighbour_sum(neighbour_sum(pressure, 1, -1), 1, -2))
    across_z = neighbour_sum(combined, 1, -1)
    force_y = 0.25 * (jnp.roll(across_z, 1, axis=-2) - across_z)
    across_y = neighbour_sum(combined, 1, -2)
    force_z = 0.25 * (jnp.roll(across_y, 1, axis=-1) - across_y)
    return jnp.stack([force_x, force_y, force_z])


def zone_divergence(velocity, upper_nodes):
    diff_x = neighbour_sum(neighbour_sum(upper_nodes[0] - velocity[0], -1, -1), -1, -2)
    sum_y = neighbour_sum(velocity[1] + upper_nodes[1], -1, -1)
    diff_y = jnp.roll(sum_y, -1, axis=-2) - sum_y
    sum_z = neighbour_sum(velocity[2] + upper_nodes[2], -1, -2)
    diff_z = jnp.roll(sum_z, -1, axis=-1) - sum_z
    return 0.25 * (diff_x + diff_y + diff_z)


def advance(pressure, velocity, stiffness, inv_mass, step_size):
    empty_plane = jnp.zeros_like(pressure[:1])
    lower_zones = jnp.concatenate([empty_plane, pressure[:-1]], axis=0)
    forces = node_forces(pressure, lower_zones)
    velocity = velocity + step_size * inv_mass * forces
    upper_nodes = jnp.concatenate([velocity[:, 1:], jnp.zeros_like(velocity[:, :1])], axis=1)
    pressure = pressure - step_size * stiffness * zone_divergence(velocity, upper_nodes)
    return pressure, velocity


def propagate(pressure, velocity, stiffness, inv_mass):
    fine_size = DT_COARSE / STEPS
    for repeat in range(STEPS):
        pressure, velocity = advance(pressure, velocity, stiffness, inv_mass, fine_size)
    return pressure, velocity


def reference(guess_pressure, guess_velocity, initial_pressure, initial_velocity, stiffness, inv_mass):
    relaxed = []
    for group in range(N_TM):
        relaxed.append(propagate(guess_pressure[group], guess_velocity[group], stiffness, inv_mass))
    corrected_p = []
    corrected_v = []
    residual_p = []
    residual_v = []
    error_p = None
    error_v = None
    for group in range(N_TM):
        if group == 0:
            start_p, start_v = initial_pressure, initial_velocity
        else:
            start_p, start_v = relaxed[group - 1]
        end_p, end_v = propagate(start_p, start_v, stiffness, inv_mass)
        resid_p = end_p - relaxed[group][0]
        resid_v = end_v - relaxed[group][1]
        if group == 0:
            error_p, error_v = resid_p, resid_v
        else:
            moved_p, moved_v = advance(error_p, error_v, stiffness, inv_mass, DT_COARSE)
            error_p = resid_p + moved_p
            error_v = resid_v + moved_v
        corrected_p.append(relaxed[group][0] + error_p)
        corrected_v.append(relaxed[group][1] + error_v)
        residual_p.append(resid_p)
        residual_v.append(resid_v)
    return (jnp.stack(corrected_p), jnp.stack(corrected_v), jnp.stack(residual_p), jnp.stack(residual_v))
```

```python
import functools

import jax
import jax.numpy as jnp
from jax import lax
from jax.experimental import pallas as pl
from jax.experimental.pallas import tpu as pltpu
from jax.sharding import PartitionSpec as P

FINE = 0.4 / 4
COARSE = 0.4
NY, NZ = 64, 128
MESH = pl.DeviceIdType.MESH
SPACE, TM = "space", "tm"
(STATIC, SPREAD, INITIAL, FINE1, FINE2, FINE3, LATE, FIRST1, FIRST2, FIRST3) = range(10)
(GUESS, EARLY, SUMS, LAST, ONCE, TWICE) = range(6)
(MASS, STIFF, RATE, BEFORE, TOTAL, FUTURE, START, RELAXED, RATE0, RATE1, BEFORE1, TOTAL1, BASE_P, BASE_X) = range(14)

SPACE_MESSAGES = {
    STATIC: (4, 5),
    SPREAD: (1, 2),
    INITIAL: (3, 4),
    FINE1: (2, 2),
    FINE2: (2, 2),
    FINE3: (2, 2),
    LATE: (2, 2),
    FIRST1: (2, 2),
    FIRST2: (2, 2),
    FIRST3: (1, 1),
}
GROUP_MESSAGES = {
    GUESS: (6, 1),
    EARLY: (5, 1),
    SUMS: (3, 1),
    LAST: (2, 1),
    ONCE: (5, 2),
    TWICE: (5, 3),
}
KEPT = {
    MASS: 5,
    STIFF: 4,
    RATE: 4,
    BEFORE: 2,
    TOTAL: 4,
    FUTURE: 4,
    START: 3,
    RELAXED: 2,
    RATE0: 4,
    RATE1: 4,
    BEFORE1: 2,
    TOTAL1: 4,
    BASE_P: 2,
    BASE_X: 3,
}


def lower_y(x):
    return pltpu.roll(x, 1, 0)


def upper_y(x):
    return pltpu.roll(x, NY - 1, 0)


def lower_z(x):
    return pltpu.roll(x, 1, 1)


def upper_z(x):
    return pltpu.roll(x, NZ - 1, 1)


def corner_forces(zones):
    parts = []
    for x in zones:
        below = lower_z(x)
        s = below + x
        t = 0.5 * (below - x)
        parts.append((s, lower_y(s), t + lower_y(t)))
    forces = []
    for (s0, r0, t0), (s1, r1, t1) in zip(parts[:-1], parts[1:]):
        forces.append((r0 - s1, s0 - r1, t0 + t1))
    return forces


def gather(less, plus, along):
    a = less + upper_y(plus)
    b = along + upper_y(along)
    return (a - b) + upper_z(a + b)


def curve(zones, mass, stiff):
    weighted = [
        (m * a, m * b, m * c) for (a, b, c), m in zip(corner_forces(zones), mass)
    ]
    out = []
    for (a0, b0, c0), (a1, b1, c1), k in zip(weighted[:-1], weighted[1:], stiff):
        out.append(k * gather(b1 - a0, a1 - b0, c0 + c1))
    return out


def spread_up(v):
    return gather(v[0] - v[1], v[0] + v[1], v[2])


def spread_down(v):
    return gather(-v[0] - v[1], v[1] - v[0], v[2])


def kernel(gp_far, gv_far, ip_far, iv_far, k_far, m_far, *rest):
    far_out, bufs = rest[:4], list(rest[4:])
    space = {}
    for name in SPACE_MESSAGES:
        space[name] = tuple(bufs.pop(0) for _ in range(4))
    group = {}
    for name in GROUP_MESSAGES:
        group[name] = tuple(bufs.pop(0) for _ in range(2))
    kept = {name: bufs.pop(0) for name in KEPT}
    near = bufs[:6]
    gp, gv, ip, iv, stiffness, inv_mass = near
    near_out = bufs[6:10]
    out_cp, out_cv, out_rp, out_rv = near_out
    space_sems, group_sems, near_sems, out_sems = bufs[10:]

    fetched = {}
    far = (gp_far, gv_far, ip_far, iv_far, k_far, m_far)
    for i in (0, 4, 5, 1, 2, 3):
        fetched[i] = pltpu.make_async_copy(far[i], near[i], near_sems.at[i])
        fetched[i].start()

    s, t = lax.axis_index(SPACE), lax.axis_index(TM)
    n_s, n_t = lax.axis_size(SPACE), lax.axis_size(TM)
    has_left, has_right = s > 0, s < n_s - 1

    def space_copy(name, right):
        i = name
        to_right, from_left, to_left, from_right = space[name]
        return pltpu.make_async_remote_copy(
            src_ref=to_right if right else to_left,
            dst_ref=from_left if right else from_right,
            send_sem=space_sems.at[i, 0 if right else 1],
            recv_sem=space_sems.at[i, 2 if right else 3],
            device_id={SPACE: s + 1 if right else s - 1},
            device_id_type=MESH,
        )

    def space_send(name):
        pl.when(has_right)(lambda: space_copy(name, True).start())
        pl.when(has_left)(lambda: space_copy(name, False).start())

    def space_wait(name):
        pl.when(has_left)(lambda: space_copy(name, True).wait_recv())
        pl.when(has_right)(lambda: space_copy(name, False).wait_recv())

    def group_copy(name):
        i = name
        ahead = GROUP_MESSAGES[name][1]
        return pltpu.make_async_remote_copy(
            src_ref=group[name][0] if name != GUESS else gv,
            dst_ref=group[name][1],
            send_sem=group_sems.at[i, 0],
            recv_sem=group_sems.at[i, 1],
            device_id={TM: t + ahead},
            device_id_type=MESH,
        )

    def group_send(name):
        pl.when(t + GROUP_MESSAGES[name][1] < n_t)(lambda: group_copy(name).start())

    def group_wait(name):
        pl.when(t >= GROUP_MESSAGES[name][1])(lambda: group_copy(name).wait_recv())

    barrier = pltpu.get_barrier_semaphore()

    def tell(**where):
        pl.semaphore_signal(barrier, inc=1, device_id=where, device_id_type=MESH)

    pl.when(has_right)(lambda: tell(space=s + 1))
    pl.when(has_left)(lambda: tell(space=s - 1))
    for back in range(1, 4):
        pl.when(t >= back)(lambda back=back: tell(tm=t - back))

    def put(ref, planes):
        for i, x in enumerate(planes):
            ref[i] = x

    def get(ref):
        return [ref[i] for i in range(ref.shape[0])]

    nothing = jnp.zeros((NY, NZ), jnp.float32)

    @pl.when(s == 0)
    def _():
        for name in SPACE_MESSAGES:
            ref = space[name][1]
            put(ref, [nothing] * ref.shape[0])

    @pl.when(s == n_s - 1)
    def _():
        for name in SPACE_MESSAGES:
            ref = space[name][3]
            put(ref, [nothing] * ref.shape[0])

    for name in (ONCE, TWICE):

        @pl.when(t < GROUP_MESSAGES[name][1])
        def _(name=name):
            put(group[name][1], [nothing] * 5)

    for i in (0, 4, 5):
        fetched[i].wait()
    put(space[STATIC][0], [gp[0, 0], gp[0, 1], stiffness[1], inv_mass[1]])
    put(space[STATIC][2], [gp[0, 0], gp[0, 1], stiffness[0], inv_mass[0], inv_mass[1]])

    peers = has_right.astype(jnp.int32) + has_left.astype(jnp.int32) + (n_t - 1 - t)
    pl.semaphore_wait(barrier, peers)

    space_send(STATIC)
    fetched[1].wait()
    v0 = [gv[0, i, 0] for i in range(3)]
    v1 = [gv[0, i, 1] for i in range(3)]
    guess_up, guess_d0 = spread_up(v0), spread_up(v1) + spread_down(v0)
    guess_d1 = spread_down(v1)
    put(space[SPREAD][0], [guess_d1])
    put(space[SPREAD][2], [guess_up, guess_d0])
    space_send(SPREAD)
    fetched[2].wait()
    fetched[3].wait()
    v0 = [iv[i, 0] for i in range(3)]
    v1 = [iv[i, 1] for i in range(3)]
    first_up, first_d0 = spread_up(v0), spread_up(v1) + spread_down(v0)
    first_d1 = spread_down(v1)
    put(space[INITIAL][0], [ip[0], ip[1], first_d1])
    put(space[INITIAL][2], [ip[0], ip[1], first_up, first_d0])
    space_send(INITIAL)
    group_send(GUESS)

    def mass():
        return get(kept[MASS])

    def stiff(scale=None):
        return get(kept[STIFF])

    def fine_pair(zones, rate):
        m, k = mass(), stiff()
        rate = [r - c for r, c in zip(rate, curve(zones, m, k))]
        p1 = [x + r for x, r in zip(zones[1:-1], rate)]
        rate2 = [r - c for r, c in zip(rate[1:3], curve(p1, m[1:4], k[1:3]))]
        p2 = [x + r for x, r in zip(p1[1:3], rate2)]
        return p1, rate, p2, rate2

    def zones_of(name, own):
        left, right = get(space[name][1]), get(space[name][3])
        return left[:2] + own + right[:2]

    def next_rate(zones, before, own):
        return [zones[1] - before[0], own[0], own[1], zones[4] - before[1]]

    space_wait(STATIC)
    left, right = get(space[STATIC][1]), get(space[STATIC][3])
    put(kept[MASS], [left[3], inv_mass[0], inv_mass[1], right[3], right[4]])
    scale = 0.125 * FINE * FINE
    raw = [left[2], stiffness[0], stiffness[1], right[2]]
    put(kept[STIFF], [scale * k for k in raw])
    zones = left[:2] + [gp[0, 0], gp[0, 1]] + right[:2]
    space_wait(SPREAD)
    left, right = get(space[SPREAD][1]), get(space[SPREAD][3])
    spread = [left[0] + guess_up, guess_d0, guess_d1 + right[0], right[1]]
    rate = [(-0.25 * FINE) * k * d for k, d in zip(raw, spread)]
    p1, rate1, p2, rate2 = fine_pair(zones, rate)
    put(space[FINE1][0], p2)
    put(space[FINE1][2], p2)
    space_send(FINE1)
    put(kept[RATE], [rate2[0], rate2[0], rate2[1], rate2[1]])
    put(kept[BEFORE], [p1[0], p1[3]])
    put(kept[TOTAL], [x + y for x, y in zip(zones[1:5], p1)])

    space_wait(INITIAL)
    left, right = get(space[INITIAL][1]), get(space[INITIAL][3])
    zones = left[:2] + [ip[0], ip[1]] + right[:2]
    raw = [k * (-0.25 * FINE / scale) for k in stiff()]
    spread = [left[2] + first_up, first_d0, first_d1 + right[2], right[3]]
    rate = [k * d for k, d in zip(raw, spread)]
    put(kept[RATE0], rate)
    p1, rate1, p2, rate2 = fine_pair(zones, rate)
    put(space[FIRST1][0], p2)
    put(space[FIRST1][2], p2)
    space_send(FIRST1)
    put(kept[RATE1], [rate2[0], rate2[0], rate2[1], rate2[1]])
    put(kept[BEFORE1], [p1[0], p1[3]])
    put(kept[TOTAL1], [x + y for x, y in zip(zones[1:5], p1)])

    space_wait(FINE1)
    zones = zones_of(FINE1, get(space[FINE1][0]))
    old = get(kept[RATE])
    rate = next_rate(zones, get(kept[BEFORE]), [old[1], old[2]])
    p1, rate1, p2, rate2 = fine_pair(zones, rate)
    put(space[FINE2][0], p2)
    put(space[FINE2][2], p2)
    space_send(FINE2)
    put(kept[RATE], [rate2[0], rate2[0], rate2[1], rate2[1]])
    put(kept[BEFORE], [p1[0], p1[3]])
    total = [x + y + z for x, y, z in zip(get(kept[TOTAL]), zones[1:5], p1)]
    put(kept[TOTAL], total)
    put(kept[START], total[:3])
    put(kept[RELAXED], p2)

    space_wait(FIRST1)
    zones = zones_of(FIRST1, get(space[FIRST1][0]))
    old = get(kept[RATE1])
    rate = next_rate(zones, get(kept[BEFORE1]), [old[1], old[2]])
    p1, rate1, p2, rate2 = fine_pair(zones, rate)
    total1 = [x + y + z for x, y, z in zip(get(kept[TOTAL1]), zones[1:5], p1)]
    put(kept[TOTAL1], [0.25 * x for x in total1])
    moved = [p2[0] + 0.25 * total1[1], p2[1] + 0.25 * total1[2]]
    put(space[FIRST2][0], moved)
    put(space[FIRST2][2], moved)
    space_send(FIRST2)

    @pl.when(t == 0)
    def _():
        put(kept[BASE_P], p2)
        put(kept[BASE_X], [0.25 * x for x in total1[:3]])
        put(group[EARLY][1], [-p2[0], -p2[1]] + total1[:3])
        put(group[SUMS][1], [nothing] * 3)
        put(group[LAST][1], p2)
        for i in range(3):
            for j in range(2):
                group[GUESS][1][0, i, j] = iv[i, j]

    put(kept[BEFORE1], p2)

    space_wait(FINE2)
    zones = zones_of(FINE2, get(space[FINE2][0]))
    old = get(kept[RATE])
    rate = next_rate(zones, get(kept[BEFORE]), [old[1], old[2]])
    p1, rate1, p2, rate2 = fine_pair(zones, rate)
    put(space[FINE3][0], p2)
    put(space[FINE3][2], p2)
    space_send(FINE3)
    ahead = [12.0 * rate[i] - 16.0 * rate1[i] - zones[i + 1] for i in (1, 2)]
    sums = [x + 4.0 * y for x, y in zip(get(kept[START]), zones[1:4])]
    put(group[EARLY][0], ahead + sums)
    group_send(EARLY)
    put(kept[FUTURE], ahead + ahead)
    put(kept[RATE], [rate2[0], rate2[0], rate2[1], rate2[1]])
    put(kept[BEFORE], [p1[0], p1[3]])
    put(kept[TOTAL], [0.25 * (y - 3.0 * x) for x, y in zip(zones[1:5], p1)])

    def coarse_pair(zones, value, source):
        m, k = mass(), [16.0 * x for x in stiff()]
        one = [x - c for x, c in zip(value, curve(zones, m, k))]
        if source is not None:
            one = [x + y for x, y in zip(one, source)]
        sums = [x + y for x, y in zip(zones[1:5], one)]
        two = [x - c for x, c in zip(one[1:3], curve(sums, m[1:4], k[1:3]))]
        if source is not None:
            two = [x + y for x, y in zip(two, source[1:3])]
        return one, sums, two

    space_wait(FIRST2)
    zones = zones_of(FIRST2, get(space[FIRST2][0]))
    x0, own = get(kept[TOTAL1]), get(kept[BEFORE1])
    value = [zones[1] - x0[0], own[0], own[1], zones[4] - x0[3]]
    source = [4.0 * x for x in get(kept[RATE0])]
    one, sums, two = coarse_pair(zones, value, source)
    third = [sums[1] + two[0], sums[2] + two[1]]
    put(space[FIRST3][0], [third[1]])
    put(space[FIRST3][2], [third[0]])
    space_send(FIRST3)

    @pl.when(t == 1)
    def _():
        put(kept[BASE_P], one[1:3])
        put(kept[BASE_X], zones[1:4])

    @pl.when(t == 2)
    def _():
        put(kept[BASE_P], two)
        put(kept[BASE_X], sums[:3])

    put(kept[BEFORE1], two)
    put(kept[RATE1], third + third)

    space_wait(FINE3)
    zones = zones_of(FINE3, get(space[FINE3][0]))
    old = get(kept[RATE])
    rate = next_rate(zones, get(kept[BEFORE]), [old[1], old[2]])
    p1, rate1, p2, rate2 = fine_pair(zones, rate)
    total = [x + 0.25 * (y + z) for x, y, z in zip(get(kept[TOTAL]), zones[1:5], p1)]
    ahead = get(kept[FUTURE])
    moved = [total[i + 1] + p2[i] + ahead[i] for i in (0, 1)]
    put(space[LATE][0], moved)
    put(space[LATE][2], moved)
    space_send(LATE)
    put(group[SUMS][0], total[:3])
    group_send(SUMS)
    put(group[LAST][0], p2)
    group_send(LAST)
    put(kept[TOTAL], total)
    put(kept[BEFORE], [p2[0] + ahead[0], p2[1] + ahead[1]])

    space_wait(FIRST3)

    @pl.when(t == 3)
    def _():
        left, right = space[FIRST3][1][0], space[FIRST3][3][0]
        own, old = get(kept[RATE1]), get(kept[BEFORE1])
        source = get(kept[RATE0])
        zones = [left, own[0], own[1], right]
        k = [16.0 * x for x in stiff()]
        change = curve(zones, mass()[1:4], k[1:3])
        put(kept[BASE_P], [old[i] + 4.0 * source[i + 1] - change[i] for i in (0, 1)])
        put(kept[BASE_X], [left, own[0], own[1]])

    space_wait(LATE)
    zones = zones_of(LATE, get(space[LATE][0]))
    x0, own = get(kept[TOTAL]), get(kept[BEFORE])
    value = [zones[1] - x0[0], own[0], own[1], zones[4] - x0[3]]
    one, sums, two = coarse_pair(zones, value, None)
    put(group[ONCE][0], zones[1:4] + one[1:3])
    group_send(ONCE)
    put(group[TWICE][0], sums[:3] + two)
    group_send(TWICE)

    def velocity(planes, scale, base, out):
        for i, (a, b, c) in enumerate(corner_forces(planes)):
            m = scale * inv_mass[i]
            out[0, 0, i] = base(0, i) + (0.5 * m) * (a + b)
            out[0, 1, i] = base(1, i) + (0.5 * m) * (a - b)
            out[0, 2, i] = base(2, i) + m * c

    stored = [
        pltpu.make_async_copy(near_out[i], far_out[i], out_sems.at[i]) for i in range(4)
    ]
    group_wait(GUESS)
    group_wait(EARLY)
    group_wait(SUMS)
    early, added = get(group[EARLY][1]), get(group[SUMS][1])
    start = get(kept[START])
    velocity(
        [early[i + 2] + 4.0 * added[i] - start[i] for i in range(3)],
        0.5 * FINE,
        lambda c, i: group[GUESS][1][0, c, i] - gv[0, c, i],
        out_rv,
    )
    stored[3].start()
    group_wait(LAST)
    last = get(group[LAST][1])
    for i in range(2):
        out_rp[0, i] = last[i] - kept[RELAXED][i]
    stored[2].start()
    group_wait(ONCE)
    group_wait(TWICE)
    once, twice = get(group[ONCE][1]), get(group[TWICE][1])
    for i in range(2):
        out_cp[0, i] = kept[BASE_P][i] + (last[i] + early[i]) + once[i + 3] + twice[i + 3]
    stored[0].start()
    velocity(
        [kept[BASE_X][i] + added[i] + once[i] + twice[i] for i in range(3)],
        0.5 * COARSE,
        lambda c, i: iv[c, i],
        out_cv,
    )
    stored[1].start()

    for name in SPACE_MESSAGES:
        pl.when(has_right)(lambda name=name: space_copy(name, True).wait_send())
        pl.when(has_left)(lambda name=name: space_copy(name, False).wait_send())
    for name, (_, ahead) in GROUP_MESSAGES.items():
        pl.when(t + ahead < n_t)(lambda name=name: group_copy(name).wait_send())
    for copy in stored:
        copy.wait()


def write_out(*refs):
    held, sems = refs[8:12], refs[12]
    order = (1, 3, 0, 2)
    fetch = [pltpu.make_async_copy(refs[i], held[i], sems.at[0, i]) for i in range(4)]
    store = [pltpu.make_async_copy(held[i], refs[i + 4], sems.at[1, i]) for i in range(4)]
    for i in order:
        fetch[i].start()
    for i in order:
        fetch[i].wait()
        store[i].start()
    for i in order:
        store[i].wait()


def on_device(*args):
    def planes(n):
        return pltpu.VMEM((n, NY, NZ), jnp.float32)

    scratch = []
    for right, left in SPACE_MESSAGES.values():
        scratch += [planes(right), planes(right), planes(left), planes(left)]
    for name, (n, _) in GROUP_MESSAGES.items():
        if name == GUESS:
            scratch += [planes(1), pltpu.VMEM((1, 3, 2, NY, NZ), jnp.float32)]
        else:
            scratch += [planes(n), planes(n)]
    scratch += [planes(n) for n in KEPT.values()]
    scratch += [pltpu.VMEM(x.shape, x.dtype) for x in args]
    field, vector = (1, 2, NY, NZ), (1, 3, 2, NY, NZ)
    scratch += [pltpu.VMEM(x, jnp.float32) for x in (field, vector, field, vector)]
    scratch += [
        pltpu.SemaphoreType.DMA((len(SPACE_MESSAGES), 4)),
        pltpu.SemaphoreType.DMA((len(GROUP_MESSAGES), 2)),
        pltpu.SemaphoreType.DMA((len(args),)),
        pltpu.SemaphoreType.DMA((4,)),
    ]
    shapes = [jax.ShapeDtypeStruct(x, jnp.float32) for x in (field, vector, field, vector)]
    results = pl.pallas_call(
        kernel,
        out_shape=shapes,
        in_specs=[pl.BlockSpec(memory_space=pltpu.HBM)] * 6,
        out_specs=[pl.BlockSpec(memory_space=pltpu.HBM)] * 4,
        scratch_shapes=scratch,
        compiler_params=pltpu.CompilerParams(
            collective_id=0, has_side_effects=True, vmem_limit_bytes=60 << 20
        ),
        cost_estimate=pl.CostEstimate(
            flops=10_000_000, bytes_accessed=2_000_000, transcendentals=0
        ),
    )(*args)
    return pl.pallas_call(
        write_out,
        out_shape=shapes,
        in_specs=[pl.BlockSpec(memory_space=pltpu.HBM)] * 4,
        out_specs=[pl.BlockSpec(memory_space=pltpu.HBM)] * 4,
        scratch_shapes=[pltpu.VMEM(x.shape, x.dtype) for x in shapes]
        + [pltpu.SemaphoreType.DMA((2, 4))],
        compiler_params=pltpu.CompilerParams(vmem_limit_bytes=60 << 20),
        cost_estimate=pl.CostEstimate(flops=0, bytes_accessed=1_000_000, transcendentals=0),
    )(*results)


def solution(mesh):
    placed = (
        P(TM, SPACE, None, None),
        P(TM, None, SPACE, None, None),
        P(SPACE, None, None),
        P(None, SPACE, None, None),
        P(SPACE, None, None),
        P(SPACE, None, None),
    )
    return jax.shard_map(
        on_device,
        mesh=mesh,
        in_specs=placed,
        out_specs=(
            P(TM, SPACE, None, None),
            P(TM, None, SPACE, None, None),
            P(TM, SPACE, None, None),
            P(TM, None, SPACE, None, None),
        ),
        check_vma=False,
    )
```

```python
import functools

import jax
import jax.numpy as jnp
from jax import lax
from jax.experimental import pallas as pl
from jax.experimental.pallas import tpu as pltpu
from jax.sharding import PartitionSpec as P

FINE = 0.4 / 4
COARSE = 0.4
NY, NZ = 64, 128
MESH = pl.DeviceIdType.MESH
SPACE, TM = "space", "tm"
(STATIC, SPREAD, INITIAL, FINE1, FINE2, FINE3, LATE, FIRST1, FIRST2, FIRST3) = range(10)
(GUESS, EARLY, SUMS, LAST, OWN, ONCE, TWICE) = range(7)
(MASS, STIFF, RATE, BEFORE, TOTAL, FUTURE, START, RELAXED, RATE0, RATE1, BEFORE1, TOTAL1, BASE_P, BASE_X) = range(14)

SPACE_MESSAGES = {
    STATIC: (4, 5),
    SPREAD: (1, 2),
    INITIAL: (3, 4),
    FINE1: (2, 2),
    FINE2: (2, 2),
    FINE3: (2, 2),
    LATE: (2, 2),
    FIRST1: (2, 2),
    FIRST2: (2, 2),
    FIRST3: (1, 1),
}
GROUP_MESSAGES = {
    GUESS: (6, 1),
    EARLY: (5, 1),
    SUMS: (3, 1),
    LAST: (2, 1),
    OWN: (2, 2),
    ONCE: (3, 2),
    TWICE: (5, 3),
}
KEPT = {
    MASS: 5,
    STIFF: 4,
    RATE: 4,
    BEFORE: 2,
    TOTAL: 4,
    FUTURE: 4,
    START: 3,
    RELAXED: 2,
    RATE0: 4,
    RATE1: 4,
    BEFORE1: 2,
    TOTAL1: 4,
    BASE_P: 2,
    BASE_X: 3,
}


def lower_y(x):
    return pltpu.roll(x, 1, 0)


def upper_y(x):
    return pltpu.roll(x, NY - 1, 0)


def lower_z(x):
    return pltpu.roll(x, 1, 1)


def upper_z(x):
    return pltpu.roll(x, NZ - 1, 1)


def corner_forces(zones):
    parts = []
    for x in zones:
        below = lower_z(x)
        s = below + x
        t = 0.5 * (below - x)
        parts.append((s, lower_y(s), t + lower_y(t)))
    forces = []
    for (s0, r0, t0), (s1, r1, t1) in zip(parts[:-1], parts[1:]):
        forces.append((r0 - s1, s0 - r1, t0 + t1))
    return forces


def gather(less, plus, along):
    a = less + upper_y(plus)
    b = along + upper_y(along)
    return (a - b) + upper_z(a + b)


def curve(zones, mass, stiff):
    weighted = [
        (m * a, m * b, m * c) for (a, b, c), m in zip(corner_forces(zones), mass)
    ]
    out = []
    for (a0, b0, c0), (a1, b1, c1), k in zip(weighted[:-1], weighted[1:], stiff):
        out.append(k * gather(b1 - a0, a1 - b0, c0 + c1))
    return out


def spread_up(v):
    return gather(v[0] - v[1], v[0] + v[1], v[2])


def spread_down(v):
    return gather(-v[0] - v[1], v[1] - v[0], v[2])


def kernel(gp_far, gv_far, ip_far, iv_far, k_far, m_far, *rest):
    (out_cp, out_cv, out_rp, out_rv), bufs = rest[:4], list(rest[4:])
    space = {}
    for name in SPACE_MESSAGES:
        space[name] = tuple(bufs.pop(0) for _ in range(4))
    group = {}
    for name in GROUP_MESSAGES:
        group[name] = tuple(bufs.pop(0) for _ in range(2))
    kept = {name: bufs.pop(0) for name in KEPT}
    near = bufs[:6]
    gp, gv, ip, iv, stiffness, inv_mass = near
    ready, space_sems, group_sems, near_sems = bufs[6:]

    s, t = lax.axis_index(SPACE), lax.axis_index(TM)
    n_s, n_t = lax.axis_size(SPACE), lax.axis_size(TM)
    has_left, has_right = s > 0, s < n_s - 1

    def space_copy(name, right):
        i = name
        to_right, from_left, to_left, from_right = space[name]
        return pltpu.make_async_remote_copy(
            src_ref=to_right if right else to_left,
            dst_ref=from_left if right else from_right,
            send_sem=space_sems.at[i, 0 if right else 1],
            recv_sem=space_sems.at[i, 2 if right else 3],
            device_id={SPACE: s + 1 if right else s - 1},
            device_id_type=MESH,
        )

    def space_send(name):
        pl.when(has_right)(lambda: space_copy(name, True).start())
        pl.when(has_left)(lambda: space_copy(name, False).start())

    def space_wait(name):
        pl.when(has_left)(lambda: space_copy(name, True).wait_recv())
        pl.when(has_right)(lambda: space_copy(name, False).wait_recv())

    def group_copy(name):
        i = name
        ahead = GROUP_MESSAGES[name][1]
        return pltpu.make_async_remote_copy(
            src_ref=group[name][0] if name != GUESS else gv,
            dst_ref=group[name][1],
            send_sem=group_sems.at[i, 0],
            recv_sem=group_sems.at[i, 1],
            device_id={TM: t + ahead},
            device_id_type=MESH,
        )

    def group_send(name):
        pl.when(t + GROUP_MESSAGES[name][1] < n_t)(lambda: group_copy(name).start())

    def group_wait(name):
        pl.when(t >= GROUP_MESSAGES[name][1])(lambda: group_copy(name).wait_recv())

    barrier = pltpu.get_barrier_semaphore()

    def tell(where):
        pl.semaphore_signal(barrier, inc=1, device_id=where, device_id_type=MESH)

    pl.when(has_right)(lambda: tell({SPACE: s + 1}))
    pl.when(has_left)(lambda: tell({SPACE: s - 1}))
    for ahead in range(1, 4):
        pl.when(t + ahead < n_t)(lambda ahead=ahead: tell({TM: t + ahead}))

    fetched = {}
    far = (gp_far, gv_far, ip_far, iv_far, k_far, m_far)
    for i in (0, 4, 5, 1, 2, 3):
        fetched[i] = pltpu.make_async_copy(far[i], near[i], near_sems.at[i])
        fetched[i].start()

    def put(ref, planes):
        for i, x in enumerate(planes):
            ref[i] = x

    def get(ref):
        return [ref[i] for i in range(ref.shape[0])]

    nothing = jnp.zeros((NY, NZ), jnp.float32)

    @pl.when(s == 0)
    def _():
        for name in SPACE_MESSAGES:
            ref = space[name][1]
            put(ref, [nothing] * ref.shape[0])

    @pl.when(s == n_s - 1)
    def _():
        for name in SPACE_MESSAGES:
            ref = space[name][3]
            put(ref, [nothing] * ref.shape[0])

    for name in (OWN, ONCE, TWICE):

        @pl.when(t < GROUP_MESSAGES[name][1])
        def _(name=name):
            put(group[name][1], [nothing] * GROUP_MESSAGES[name][0])

    for i in (0, 4, 5):
        fetched[i].wait()
    put(space[STATIC][0], [gp[0, 0], gp[0, 1], stiffness[1], inv_mass[1]])
    put(space[STATIC][2], [gp[0, 0], gp[0, 1], stiffness[0], inv_mass[0], inv_mass[1]])

    fetched[1].wait()
    v0 = [gv[0, i, 0] for i in range(3)]
    v1 = [gv[0, i, 1] for i in range(3)]
    guess_up, guess_d0 = spread_up(v0), spread_up(v1) + spread_down(v0)
    guess_d1 = spread_down(v1)
    put(space[SPREAD][0], [guess_d1])
    put(space[SPREAD][2], [guess_up, guess_d0])

    peers = has_right.astype(jnp.int32) + has_left.astype(jnp.int32) + t
    pl.semaphore_wait(barrier, peers)
    space_send(STATIC)
    space_send(SPREAD)
    for back in range(1, 4):

        @pl.when(t >= back)
        def _(back=back):
            pl.semaphore_signal(
                ready.at[back - 1], inc=1, device_id={TM: t - back}, device_id_type=MESH
            )

    fetched[2].wait()
    fetched[3].wait()
    v0 = [iv[i, 0] for i in range(3)]
    v1 = [iv[i, 1] for i in range(3)]
    first_up, first_d0 = spread_up(v0), spread_up(v1) + spread_down(v0)
    first_d1 = spread_down(v1)
    put(space[INITIAL][0], [ip[0], ip[1], first_d1])
    put(space[INITIAL][2], [ip[0], ip[1], first_up, first_d0])
    space_send(INITIAL)

    def mass():
        return get(kept[MASS])

    def stiff(scale=None):
        return get(kept[STIFF])

    def fine_pair(zones, rate):
        m, k = mass(), stiff()
        rate = [r - c for r, c in zip(rate, curve(zones, m, k))]
        p1 = [x + r for x, r in zip(zones[1:-1], rate)]
        rate2 = [r - c for r, c in zip(rate[1:3], curve(p1, m[1:4], k[1:3]))]
        p2 = [x + r for x, r in zip(p1[1:3], rate2)]
        return p1, rate, p2, rate2

    def zones_of(name, own):
        left, right = get(space[name][1]), get(space[name][3])
        return left[:2] + own + right[:2]

    def next_rate(zones, before, own):
        return [zones[1] - before[0], own[0], own[1], zones[4] - before[1]]

    space_wait(STATIC)
    left, right = get(space[STATIC][1]), get(space[STATIC][3])
    put(kept[MASS], [left[3], inv_mass[0], inv_mass[1], right[3], right[4]])
    scale = 0.125 * FINE * FINE
    raw = [left[2], stiffness[0], stiffness[1], right[2]]
    put(kept[STIFF], [scale * k for k in raw])
    zones = left[:2] + [gp[0, 0], gp[0, 1]] + right[:2]
    space_wait(SPREAD)
    left, right = get(space[SPREAD][1]), get(space[SPREAD][3])
    spread = [left[0] + guess_up, guess_d0, guess_d1 + right[0], right[1]]
    rate = [(-0.25 * FINE) * k * d for k, d in zip(raw, spread)]
    p1, rate1, p2, rate2 = fine_pair(zones, rate)
    put(space[FINE1][0], p2)
    put(space[FINE1][2], p2)
    space_send(FINE1)
    put(kept[RATE], [rate2[0], rate2[0], rate2[1], rate2[1]])
    put(kept[BEFORE], [p1[0], p1[3]])
    put(kept[TOTAL], [x + y for x, y in zip(zones[1:5], p1)])

    space_wait(INITIAL)
    left, right = get(space[INITIAL][1]), get(space[INITIAL][3])
    zones = left[:2] + [ip[0], ip[1]] + right[:2]
    raw = [k * (-0.25 * FINE / scale) for k in stiff()]
    spread = [left[2] + first_up, first_d0, first_d1 + right[2], right[3]]
    rate = [k * d for k, d in zip(raw, spread)]
    put(kept[RATE0], rate)
    p1, rate1, p2, rate2 = fine_pair(zones, rate)
    put(space[FIRST1][0], p2)
    put(space[FIRST1][2], p2)
    space_send(FIRST1)
    for ahead in range(1, 4):
        pl.when(t + ahead < n_t)(lambda ahead=ahead: pl.semaphore_wait(ready.at[ahead - 1], 1))
    group_send(GUESS)
    put(kept[RATE1], [rate2[0], rate2[0], rate2[1], rate2[1]])
    put(kept[BEFORE1], [p1[0], p1[3]])
    put(kept[TOTAL1], [x + y for x, y in zip(zones[1:5], p1)])

    space_wait(FINE1)
    zones = zones_of(FINE1, get(space[FINE1][0]))
    old = get(kept[RATE])
    rate = next_rate(zones, get(kept[BEFORE]), [old[1], old[2]])
    p1, rate1, p2, rate2 = fine_pair(zones, rate)
    put(space[FINE2][0], p2)
    put(space[FINE2][2], p2)
    space_send(FINE2)
    put(kept[RATE], [rate2[0], rate2[0], rate2[1], rate2[1]])
    put(kept[BEFORE], [p1[0], p1[3]])
    total = [x + y + z for x, y, z in zip(get(kept[TOTAL]), zones[1:5], p1)]
    put(kept[TOTAL], total)
    put(kept[START], total[:3])
    put(kept[RELAXED], p2)

    space_wait(FIRST1)
    zones = zones_of(FIRST1, get(space[FIRST1][0]))
    old = get(kept[RATE1])
    rate = next_rate(zones, get(kept[BEFORE1]), [old[1], old[2]])
    p1, rate1, p2, rate2 = fine_pair(zones, rate)
    total1 = [x + y + z for x, y, z in zip(get(kept[TOTAL1]), zones[1:5], p1)]
    put(kept[TOTAL1], [0.25 * x for x in total1])
    moved = [p2[0] + 0.25 * total1[1], p2[1] + 0.25 * total1[2]]
    put(space[FIRST2][0], moved)
    put(space[FIRST2][2], moved)
    space_send(FIRST2)

    @pl.when(t == 0)
    def _():
        put(kept[BASE_P], p2)
        put(kept[BASE_X], [0.25 * x for x in total1[:3]])
        put(group[EARLY][1], [-p2[0], -p2[1]] + total1[:3])
        put(group[SUMS][1], [nothing] * 3)
        put(group[LAST][1], p2)
        for i in range(3):
            for j in range(2):
                group[GUESS][1][0, i, j] = iv[i, j]

    put(kept[BEFORE1], p2)

    space_wait(FINE2)
    zones = zones_of(FINE2, get(space[FINE2][0]))
    old = get(kept[RATE])
    rate = next_rate(zones, get(kept[BEFORE]), [old[1], old[2]])
    p1, rate1, p2, rate2 = fine_pair(zones, rate)
    put(space[FINE3][0], p2)
    put(space[FINE3][2], p2)
    space_send(FINE3)
    ahead = [12.0 * rate[i] - 16.0 * rate1[i] - zones[i + 1] for i in (1, 2)]
    sums = [x + 4.0 * y for x, y in zip(get(kept[START]), zones[1:4])]
    put(group[EARLY][0], ahead + sums)
    group_send(EARLY)
    put(kept[FUTURE], ahead + ahead)
    put(kept[RATE], [rate2[0], rate2[0], rate2[1], rate2[1]])
    put(kept[BEFORE], [p1[0], p1[3]])
    put(kept[TOTAL], [0.25 * (y - 3.0 * x) for x, y in zip(zones[1:5], p1)])

    def coarse_pair(zones, value, source):
        m, k = mass(), [16.0 * x for x in stiff()]
        one = [x - c for x, c in zip(value, curve(zones, m, k))]
        if source is not None:
            one = [x + y for x, y in zip(one, source)]
        sums = [x + y for x, y in zip(zones[1:5], one)]
        two = [x - c for x, c in zip(one[1:3], curve(sums, m[1:4], k[1:3]))]
        if source is not None:
            two = [x + y for x, y in zip(two, source[1:3])]
        return one, sums, two

    space_wait(FIRST2)
    zones = zones_of(FIRST2, get(space[FIRST2][0]))
    x0, own = get(kept[TOTAL1]), get(kept[BEFORE1])
    value = [zones[1] - x0[0], own[0], own[1], zones[4] - x0[3]]
    source = [4.0 * x for x in get(kept[RATE0])]
    one, sums, two = coarse_pair(zones, value, source)
    third = [sums[1] + two[0], sums[2] + two[1]]
    put(space[FIRST3][0], [third[1]])
    put(space[FIRST3][2], [third[0]])
    space_send(FIRST3)

    @pl.when(t == 1)
    def _():
        put(kept[BASE_P], one[1:3])
        put(kept[BASE_X], zones[1:4])

    @pl.when(t == 2)
    def _():
        put(kept[BASE_P], two)
        put(kept[BASE_X], sums[:3])

    put(kept[BEFORE1], two)
    put(kept[RATE1], third + third)

    space_wait(FINE3)
    zones = zones_of(FINE3, get(space[FINE3][0]))
    old = get(kept[RATE])
    rate = next_rate(zones, get(kept[BEFORE]), [old[1], old[2]])
    p1, rate1, p2, rate2 = fine_pair(zones, rate)
    total = [x + 0.25 * (y + z) for x, y, z in zip(get(kept[TOTAL]), zones[1:5], p1)]
    ahead = get(kept[FUTURE])
    moved = [total[i + 1] + p2[i] + ahead[i] for i in (0, 1)]
    put(space[LATE][0], moved)
    put(space[LATE][2], moved)
    space_send(LATE)
    put(group[SUMS][0], total[:3])
    group_send(SUMS)
    put(group[LAST][0], p2)
    group_send(LAST)
    put(group[OWN][0], moved)
    group_send(OWN)
    put(kept[TOTAL], total)
    put(kept[BEFORE], [p2[0] + ahead[0], p2[1] + ahead[1]])

    space_wait(FIRST3)

    @pl.when(t == 3)
    def _():
        left, right = space[FIRST3][1][0], space[FIRST3][3][0]
        own, old = get(kept[RATE1]), get(kept[BEFORE1])
        source = get(kept[RATE0])
        zones = [left, own[0], own[1], right]
        k = [16.0 * x for x in stiff()]
        change = curve(zones, mass()[1:4], k[1:3])
        put(kept[BASE_P], [old[i] + 4.0 * source[i + 1] - change[i] for i in (0, 1)])
        put(kept[BASE_X], [left, own[0], own[1]])

    space_wait(LATE)
    zones = zones_of(LATE, get(space[LATE][0]))
    x0, own = get(kept[TOTAL]), get(kept[BEFORE])
    value = [zones[1] - x0[0], own[0], own[1], zones[4] - x0[3]]
    one, sums, two = coarse_pair(zones, value, None)
    put(group[ONCE][0], [zones[1]] + one[1:3])
    group_send(ONCE)
    put(group[TWICE][0], sums[:3] + two)
    group_send(TWICE)

    def velocity(planes, scale, base, out):
        for i, (a, b, c) in enumerate(corner_forces(planes)):
            m = scale * inv_mass[i]
            out[0, 0, i] = base(0, i) + (0.5 * m) * (a + b)
            out[0, 1, i] = base(1, i) + (0.5 * m) * (a - b)
            out[0, 2, i] = base(2, i) + m * c

    group_wait(GUESS)
    group_wait(EARLY)
    group_wait(SUMS)
    early, added = get(group[EARLY][1]), get(group[SUMS][1])
    start = get(kept[START])
    velocity(
        [early[i + 2] + 4.0 * added[i] - start[i] for i in range(3)],
        0.5 * FINE,
        lambda c, i: group[GUESS][1][0, c, i] - gv[0, c, i],
        out_rv,
    )
    group_wait(LAST)
    last = get(group[LAST][1])
    for i in range(2):
        out_rp[0, i] = last[i] - kept[RELAXED][i]
    group_wait(OWN)
    group_wait(ONCE)
    group_wait(TWICE)
    once, twice = get(group[ONCE][1]), get(group[TWICE][1])
    once = once[:1] + get(group[OWN][1]) + once[1:]
    for i in range(2):
        out_cp[0, i] = kept[BASE_P][i] + (last[i] + early[i]) + once[i + 3] + twice[i + 3]
    velocity(
        [kept[BASE_X][i] + added[i] + once[i] + twice[i] for i in range(3)],
        0.5 * COARSE,
        lambda c, i: iv[c, i],
        out_cv,
    )

    for name in SPACE_MESSAGES:
        pl.when(has_right)(lambda name=name: space_copy(name, True).wait_send())
        pl.when(has_left)(lambda name=name: space_copy(name, False).wait_send())
    for name, (_, ahead) in GROUP_MESSAGES.items():
        pl.when(t + ahead < n_t)(lambda name=name: group_copy(name).wait_send())


def write_out(*refs):
    store = [pltpu.make_async_copy(refs[i], refs[i + 4], refs[8].at[i]) for i in range(4)]
    for copy in store:
        copy.start()
    for copy in store:
        copy.wait()


def on_device(*args):
    def planes(n):
        return pltpu.VMEM((n, NY, NZ), jnp.float32)

    scratch = []
    for right, left in SPACE_MESSAGES.values():
        scratch += [planes(right), planes(right), planes(left), planes(left)]
    for name, (n, _) in GROUP_MESSAGES.items():
        if name == GUESS:
            scratch += [planes(1), pltpu.VMEM((1, 3, 2, NY, NZ), jnp.float32)]
        else:
            scratch += [planes(n), planes(n)]
    scratch += [planes(n) for n in KEPT.values()]
    scratch += [pltpu.VMEM(x.shape, x.dtype) for x in args]
    field, vector = (1, 2, NY, NZ), (1, 3, 2, NY, NZ)
    scratch += [
        pltpu.SemaphoreType.REGULAR((3,)),
        pltpu.SemaphoreType.DMA((len(SPACE_MESSAGES), 4)),
        pltpu.SemaphoreType.DMA((len(GROUP_MESSAGES), 2)),
        pltpu.SemaphoreType.DMA((len(args),)),
    ]
    shapes = [jax.ShapeDtypeStruct(x, jnp.float32) for x in (field, vector, field, vector)]
    results = pl.pallas_call(
        kernel,
        out_shape=[pltpu.VMEM(x.shape, x.dtype) for x in shapes],
        in_specs=[pl.BlockSpec(memory_space=pltpu.HBM)] * 6,
        out_specs=[pl.BlockSpec(memory_space=pltpu.VMEM)] * 4,
        scratch_shapes=scratch,
        compiler_params=pltpu.CompilerParams(
            collective_id=0, has_side_effects=True, vmem_limit_bytes=24 << 20
        ),
        cost_estimate=pl.CostEstimate(
            flops=10_000_000, bytes_accessed=2_000_000, transcendentals=0
        ),
    )(*[pltpu.with_memory_space_constraint(x, pltpu.HBM) for x in args])
    return pl.pallas_call(
        write_out,
        out_shape=shapes,
        in_specs=[pl.BlockSpec(memory_space=pltpu.VMEM)] * 4,
        out_specs=[pl.BlockSpec(memory_space=pltpu.HBM)] * 4,
        scratch_shapes=[pltpu.SemaphoreType.DMA((4,))],
        compiler_params=pltpu.CompilerParams(vmem_limit_bytes=24 << 20),
        cost_estimate=pl.CostEstimate(flops=0, bytes_accessed=1_000_000, transcendentals=0),
    )(*results)


def solution(mesh):
    placed = (
        P(TM, SPACE, None, None),
        P(TM, None, SPACE, None, None),
        P(SPACE, None, None),
        P(None, SPACE, None, None),
        P(SPACE, None, None),
        P(SPACE, None, None),
    )
    return jax.shard_map(
        on_device,
        mesh=mesh,
        in_specs=placed,
        out_specs=(
            P(TM, SPACE, None, None),
            P(TM, None, SPACE, None, None),
            P(TM, SPACE, None, None),
            P(TM, None, SPACE, None, None),
        ),
        check_vma=False,
    )
```

```python
import functools

import jax
import jax.numpy as jnp
from jax import lax
from jax.experimental import pallas as pl
from jax.experimental.pallas import tpu as pltpu
from jax.sharding import PartitionSpec as P

FINE = 0.4 / 4
COARSE = 0.4
NY, NZ = 64, 128
MESH = pl.DeviceIdType.MESH
SPACE, TM = "space", "tm"
(STATIC, SPREAD, INITIAL, FINE1, FINE2, FINE3, LATE, FIRST1, FIRST2, FIRST3) = range(10)
(GUESS, MID, EARLY, SUMS, LAST, RELAY, ONCE, TWICE, THEN) = range(9)
(MASS, STIFF, RATE, BEFORE, TOTAL, FUTURE, START, RELAXED, RATE0, RATE1, BEFORE1, TOTAL1, BASE_P, BASE_X) = range(14)

SPACE_MESSAGES = {
    STATIC: (4, 5),
    SPREAD: (1, 2),
    INITIAL: (3, 4),
    FINE1: (2, 2),
    FINE2: (2, 2),
    FINE3: (2, 2),
    LATE: (2, 2),
    FIRST1: (2, 2),
    FIRST2: (2, 2),
    FIRST3: (1, 1),
}
GROUP_MESSAGES = {
    GUESS: (6, 1, 0),
    MID: (2, 1, 0),
    EARLY: (3, 1, 0),
    SUMS: (3, 1, 0),
    LAST: (2, 1, 0),
    RELAY: (2, 1, 1),
    ONCE: (3, 2, 0),
    TWICE: (3, 3, 0),
    THEN: (2, 3, 0),
}
KEPT = {
    MASS: 5,
    STIFF: 4,
    RATE: 4,
    BEFORE: 2,
    TOTAL: 4,
    FUTURE: 4,
    START: 3,
    RELAXED: 2,
    RATE0: 4,
    RATE1: 4,
    BEFORE1: 2,
    TOTAL1: 4,
    BASE_P: 2,
    BASE_X: 3,
}


def lower_y(x):
    return pltpu.roll(x, 1, 0)


def upper_y(x):
    return pltpu.roll(x, NY - 1, 0)


def lower_z(x):
    return pltpu.roll(x, 1, 1)


def upper_z(x):
    return pltpu.roll(x, NZ - 1, 1)


def corner_forces(zones):
    parts = []
    for x in zones:
        below = lower_z(x)
        s = below + x
        t = 0.5 * (below - x)
        parts.append((s, lower_y(s), t + lower_y(t)))
    forces = []
    for (s0, r0, t0), (s1, r1, t1) in zip(parts[:-1], parts[1:]):
        forces.append((r0 - s1, s0 - r1, t0 + t1))
    return forces


def gather(less, plus, along):
    a = less + upper_y(plus)
    b = along + upper_y(along)
    return (a - b) + upper_z(a + b)


def curve(zones, mass, stiff):
    weighted = [
        (m * a, m * b, m * c) for (a, b, c), m in zip(corner_forces(zones), mass)
    ]
    out = []
    for (a0, b0, c0), (a1, b1, c1), k in zip(weighted[:-1], weighted[1:], stiff):
        out.append(k * gather(b1 - a0, a1 - b0, c0 + c1))
    return out


def spread_up(v):
    return gather(v[0] - v[1], v[0] + v[1], v[2])


def spread_down(v):
    return gather(-v[0] - v[1], v[1] - v[0], v[2])


def kernel(gp_far, gv_far, ip_far, iv_far, k_far, m_far, *rest):
    (out_cp, out_cv, out_rp, out_rv), bufs = rest[:4], list(rest[4:])
    space = {}
    for name in SPACE_MESSAGES:
        space[name] = tuple(bufs.pop(0) for _ in range(4))
    group = {}
    for name in GROUP_MESSAGES:
        group[name] = tuple(bufs.pop(0) for _ in range(2))
    kept = {name: bufs.pop(0) for name in KEPT}
    near = bufs[:6]
    gp, gv, ip, iv, stiffness, inv_mass = near
    ready, space_sems, group_sems, near_sems = bufs[6:]

    s, t = lax.axis_index(SPACE), lax.axis_index(TM)
    n_s, n_t = lax.axis_size(SPACE), lax.axis_size(TM)
    has_left, has_right = s > 0, s < n_s - 1

    def space_copy(name, right):
        i = name
        to_right, from_left, to_left, from_right = space[name]
        return pltpu.make_async_remote_copy(
            src_ref=to_right if right else to_left,
            dst_ref=from_left if right else from_right,
            send_sem=space_sems.at[i, 0 if right else 1],
            recv_sem=space_sems.at[i, 2 if right else 3],
            device_id={SPACE: s + 1 if right else s - 1},
            device_id_type=MESH,
        )

    def space_send(name):
        pl.when(has_right)(lambda: space_copy(name, True).start())
        pl.when(has_left)(lambda: space_copy(name, False).start())

    def space_wait(name):
        pl.when(has_left)(lambda: space_copy(name, True).wait_recv())
        pl.when(has_right)(lambda: space_copy(name, False).wait_recv())

    def group_copy(name):
        i = name
        ahead = GROUP_MESSAGES[name][1]
        return pltpu.make_async_remote_copy(
            src_ref=group[name][0] if name != GUESS else gv,
            dst_ref=group[name][1],
            send_sem=group_sems.at[i, 0],
            recv_sem=group_sems.at[i, 1],
            device_id={TM: t + ahead},
            device_id_type=MESH,
        )

    def sends_on(name):
        _, ahead, first = GROUP_MESSAGES[name]
        return (t >= first) & (t + ahead < n_t)

    def hears(name):
        _, ahead, first = GROUP_MESSAGES[name]
        return t >= ahead + first

    def heard(ahead):
        pl.when(t + ahead < n_t)(lambda: pl.semaphore_wait(ready.at[ahead - 1], 1))

    def group_send(name):
        pl.when(sends_on(name))(lambda: group_copy(name).start())

    def group_wait(name):
        pl.when(hears(name))(lambda: group_copy(name).wait_recv())

    barrier = pltpu.get_barrier_semaphore()

    def tell(where):
        pl.semaphore_signal(barrier, inc=1, device_id=where, device_id_type=MESH)

    pl.when(has_right)(lambda: tell({SPACE: s + 1}))
    pl.when(has_left)(lambda: tell({SPACE: s - 1}))
    for ahead in range(1, 4):
        pl.when(t + ahead < n_t)(lambda ahead=ahead: tell({TM: t + ahead}))

    fetched = {}
    far = (gp_far, gv_far, ip_far, iv_far, k_far, m_far)
    for i in (0, 4, 5, 1, 2, 3):
        fetched[i] = pltpu.make_async_copy(far[i], near[i], near_sems.at[i])
        fetched[i].start()

    def put(ref, planes):
        for i, x in enumerate(planes):
            ref[i] = x

    def get(ref):
        return [ref[i] for i in range(ref.shape[0])]

    nothing = jnp.zeros((NY, NZ), jnp.float32)

    @pl.when(s == 0)
    def _():
        for name in SPACE_MESSAGES:
            ref = space[name][1]
            put(ref, [nothing] * ref.shape[0])

    @pl.when(s == n_s - 1)
    def _():
        for name in SPACE_MESSAGES:
            ref = space[name][3]
            put(ref, [nothing] * ref.shape[0])

    for name in (RELAY, ONCE, TWICE, THEN):

        @pl.when(jnp.logical_not(hears(name)))
        def _(name=name):
            put(group[name][1], [nothing] * GROUP_MESSAGES[name][0])

    for i in (0, 4, 5):
        fetched[i].wait()
    put(space[STATIC][0], [gp[0, 0], gp[0, 1], stiffness[1], inv_mass[1]])
    put(space[STATIC][2], [gp[0, 0], gp[0, 1], stiffness[0], inv_mass[0], inv_mass[1]])

    fetched[1].wait()
    v0 = [gv[0, i, 0] for i in range(3)]
    v1 = [gv[0, i, 1] for i in range(3)]
    guess_up, guess_d0 = spread_up(v0), spread_up(v1) + spread_down(v0)
    guess_d1 = spread_down(v1)
    put(space[SPREAD][0], [guess_d1])
    put(space[SPREAD][2], [guess_up, guess_d0])

    peers = has_right.astype(jnp.int32) + has_left.astype(jnp.int32) + t
    pl.semaphore_wait(barrier, peers)
    space_send(STATIC)
    space_send(SPREAD)
    for back in range(1, 4):

        @pl.when(t >= back)
        def _(back=back):
            pl.semaphore_signal(
                ready.at[back - 1], inc=1, device_id={TM: t - back}, device_id_type=MESH
            )

    fetched[2].wait()
    fetched[3].wait()
    v0 = [iv[i, 0] for i in range(3)]
    v1 = [iv[i, 1] for i in range(3)]
    first_up, first_d0 = spread_up(v0), spread_up(v1) + spread_down(v0)
    first_d1 = spread_down(v1)
    put(space[INITIAL][0], [ip[0], ip[1], first_d1])
    put(space[INITIAL][2], [ip[0], ip[1], first_up, first_d0])
    space_send(INITIAL)

    def mass():
        return get(kept[MASS])

    def stiff(scale=None):
        return get(kept[STIFF])

    def fine_pair(zones, rate):
        m, k = mass(), stiff()
        rate = [r - c for r, c in zip(rate, curve(zones, m, k))]
        p1 = [x + r for x, r in zip(zones[1:-1], rate)]
        rate2 = [r - c for r, c in zip(rate[1:3], curve(p1, m[1:4], k[1:3]))]
        p2 = [x + r for x, r in zip(p1[1:3], rate2)]
        return p1, rate, p2, rate2

    def zones_of(name, own):
        left, right = get(space[name][1]), get(space[name][3])
        return left[:2] + own + right[:2]

    def next_rate(zones, before, own):
        return [zones[1] - before[0], own[0], own[1], zones[4] - before[1]]

    space_wait(STATIC)
    left, right = get(space[STATIC][1]), get(space[STATIC][3])
    put(kept[MASS], [left[3], inv_mass[0], inv_mass[1], right[3], right[4]])
    scale = 0.125 * FINE * FINE
    raw = [left[2], stiffness[0], stiffness[1], right[2]]
    put(kept[STIFF], [scale * k for k in raw])
    zones = left[:2] + [gp[0, 0], gp[0, 1]] + right[:2]
    space_wait(SPREAD)
    left, right = get(space[SPREAD][1]), get(space[SPREAD][3])
    spread = [left[0] + guess_up, guess_d0, guess_d1 + right[0], right[1]]
    rate = [(-0.25 * FINE) * k * d for k, d in zip(raw, spread)]
    p1, rate1, p2, rate2 = fine_pair(zones, rate)
    put(space[FINE1][0], p2)
    put(space[FINE1][2], p2)
    space_send(FINE1)
    heard(1)
    group_send(GUESS)
    put(kept[RATE], [rate2[0], rate2[0], rate2[1], rate2[1]])
    put(kept[BEFORE], [p1[0], p1[3]])
    put(kept[TOTAL], [x + y for x, y in zip(zones[1:5], p1)])

    space_wait(INITIAL)
    left, right = get(space[INITIAL][1]), get(space[INITIAL][3])
    zones = left[:2] + [ip[0], ip[1]] + right[:2]
    raw = [k * (-0.25 * FINE / scale) for k in stiff()]
    spread = [left[2] + first_up, first_d0, first_d1 + right[2], right[3]]
    rate = [k * d for k, d in zip(raw, spread)]
    put(kept[RATE0], rate)
    p1, rate1, p2, rate2 = fine_pair(zones, rate)
    put(space[FIRST1][0], p2)
    put(space[FIRST1][2], p2)
    space_send(FIRST1)
    put(kept[RATE1], [rate2[0], rate2[0], rate2[1], rate2[1]])
    put(kept[BEFORE1], [p1[0], p1[3]])
    put(kept[TOTAL1], [x + y for x, y in zip(zones[1:5], p1)])

    space_wait(FINE1)
    zones = zones_of(FINE1, get(space[FINE1][0]))
    old = get(kept[RATE])
    rate = next_rate(zones, get(kept[BEFORE]), [old[1], old[2]])
    p1, rate1, p2, rate2 = fine_pair(zones, rate)
    put(space[FINE2][0], p2)
    put(space[FINE2][2], p2)
    space_send(FINE2)
    put(kept[RATE], [rate2[0], rate2[0], rate2[1], rate2[1]])
    put(kept[BEFORE], [p1[0], p1[3]])
    total = [x + y + z for x, y, z in zip(get(kept[TOTAL]), zones[1:5], p1)]
    put(kept[TOTAL], total)
    put(kept[START], total[:3])
    put(kept[RELAXED], p2)
    put(group[MID][0], [total[1] + 4.0 * p2[0], total[2] + 4.0 * p2[1]])
    group_send(MID)

    space_wait(FIRST1)
    zones = zones_of(FIRST1, get(space[FIRST1][0]))
    old = get(kept[RATE1])
    rate = next_rate(zones, get(kept[BEFORE1]), [old[1], old[2]])
    p1, rate1, p2, rate2 = fine_pair(zones, rate)
    total1 = [x + y + z for x, y, z in zip(get(kept[TOTAL1]), zones[1:5], p1)]
    put(kept[TOTAL1], [0.25 * x for x in total1])
    moved = [p2[0] + 0.25 * total1[1], p2[1] + 0.25 * total1[2]]
    put(space[FIRST2][0], moved)
    put(space[FIRST2][2], moved)
    space_send(FIRST2)

    @pl.when(t == 0)
    def _():
        put(kept[BASE_P], p2)
        put(kept[BASE_X], [0.25 * x for x in total1[:3]])
        put(group[EARLY][1], [-p2[0], -p2[1], total1[0]])
        put(group[MID][1], total1[1:3])
        put(group[SUMS][1], [nothing] * 3)
        put(group[LAST][1], p2)
        for i in range(3):
            for j in range(2):
                group[GUESS][1][0, i, j] = iv[i, j]

    put(kept[BEFORE1], p2)

    space_wait(FINE2)
    zones = zones_of(FINE2, get(space[FINE2][0]))
    old = get(kept[RATE])
    rate = next_rate(zones, get(kept[BEFORE]), [old[1], old[2]])
    p1, rate1, p2, rate2 = fine_pair(zones, rate)
    put(space[FINE3][0], p2)
    put(space[FINE3][2], p2)
    space_send(FINE3)
    ahead = [12.0 * rate[i] - 16.0 * rate1[i] - zones[i + 1] for i in (1, 2)]
    put(group[EARLY][0], ahead + [kept[START][0] + 4.0 * zones[1]])
    group_send(EARLY)
    put(kept[FUTURE], ahead + ahead)
    put(kept[RATE], [rate2[0], rate2[0], rate2[1], rate2[1]])
    put(kept[BEFORE], [p1[0], p1[3]])
    put(kept[TOTAL], [0.25 * (y - 3.0 * x) for x, y in zip(zones[1:5], p1)])

    def coarse_first(zones, value, source):
        k = [16.0 * x for x in stiff()]
        one = [x - c for x, c in zip(value, curve(zones, mass(), k))]
        if source is not None:
            one = [x + y for x, y in zip(one, source)]
        return one, [x + y for x, y in zip(zones[1:5], one)]

    def coarse_second(one, sums, source):
        k = [16.0 * x for x in stiff()]
        two = [x - c for x, c in zip(one[1:3], curve(sums, mass()[1:4], k[1:3]))]
        if source is not None:
            two = [x + y for x, y in zip(two, source[1:3])]
        return two

    space_wait(FIRST2)
    zones = zones_of(FIRST2, get(space[FIRST2][0]))
    x0, own = get(kept[TOTAL1]), get(kept[BEFORE1])
    value = [zones[1] - x0[0], own[0], own[1], zones[4] - x0[3]]
    source = [4.0 * x for x in get(kept[RATE0])]
    one, sums = coarse_first(zones, value, source)
    two = coarse_second(one, sums, source)
    third = [sums[1] + two[0], sums[2] + two[1]]
    put(space[FIRST3][0], [third[1]])
    put(space[FIRST3][2], [third[0]])
    space_send(FIRST3)

    @pl.when(t == 1)
    def _():
        put(kept[BASE_P], one[1:3])
        put(kept[BASE_X], zones[1:4])

    @pl.when(t == 2)
    def _():
        put(kept[BASE_P], two)
        put(kept[BASE_X], sums[:3])

    put(kept[BEFORE1], two)
    put(kept[RATE1], third + third)

    space_wait(FINE3)
    zones = zones_of(FINE3, get(space[FINE3][0]))
    old = get(kept[RATE])
    rate = next_rate(zones, get(kept[BEFORE]), [old[1], old[2]])
    p1, rate1, p2, rate2 = fine_pair(zones, rate)
    total = [x + 0.25 * (y + z) for x, y, z in zip(get(kept[TOTAL]), zones[1:5], p1)]
    ahead = get(kept[FUTURE])
    moved = [total[i + 1] + p2[i] + ahead[i] for i in (0, 1)]
    put(space[LATE][0], moved)
    put(space[LATE][2], moved)
    space_send(LATE)
    put(group[SUMS][0], total[:3])
    group_send(SUMS)
    put(group[LAST][0], p2)
    group_send(LAST)
    put(kept[TOTAL], total)
    put(kept[BEFORE], [p2[0] + ahead[0], p2[1] + ahead[1]])

    space_wait(FIRST3)

    @pl.when(t == 3)
    def _():
        left, right = space[FIRST3][1][0], space[FIRST3][3][0]
        own, old = get(kept[RATE1]), get(kept[BEFORE1])
        source = get(kept[RATE0])
        zones = [left, own[0], own[1], right]
        k = [16.0 * x for x in stiff()]
        change = curve(zones, mass()[1:4], k[1:3])
        put(kept[BASE_P], [old[i] + 4.0 * source[i + 1] - change[i] for i in (0, 1)])
        put(kept[BASE_X], [left, own[0], own[1]])

    space_wait(LATE)
    zones = zones_of(LATE, get(space[LATE][0]))
    x0, own = get(kept[TOTAL]), get(kept[BEFORE])
    value = [zones[1] - x0[0], own[0], own[1], zones[4] - x0[3]]
    one, sums = coarse_first(zones, value, None)
    put(group[TWICE][0], sums[:3])
    heard(3)
    group_send(TWICE)
    put(group[ONCE][0], [zones[1]] + one[1:3])
    heard(2)
    group_send(ONCE)
    put(group[THEN][0], coarse_second(one, sums, None))
    group_send(THEN)

    group_wait(EARLY)
    group_wait(SUMS)
    group_wait(LAST)
    early, added, last = get(group[EARLY][1]), get(group[SUMS][1]), get(group[LAST][1])
    put(group[RELAY][0], [added[i + 1] + (last[i] + early[i]) for i in (0, 1)])
    group_send(RELAY)

    def velocity(planes, scale, base, out):
        for i, (a, b, c) in enumerate(corner_forces(planes)):
            m = scale * inv_mass[i]
            out[0, 0, i] = base(0, i) + (0.5 * m) * (a + b)
            out[0, 1, i] = base(1, i) + (0.5 * m) * (a - b)
            out[0, 2, i] = base(2, i) + m * c

    group_wait(GUESS)
    group_wait(MID)
    early, added, last = get(group[EARLY][1]), get(group[SUMS][1]), get(group[LAST][1])
    whole = early[2:] + get(group[MID][1])
    start = get(kept[START])
    velocity(
        [whole[i] + 4.0 * added[i] - start[i] for i in range(3)],
        0.5 * FINE,
        lambda c, i: group[GUESS][1][0, c, i] - gv[0, c, i],
        out_rv,
    )
    for i in range(2):
        out_rp[0, i] = last[i] - kept[RELAXED][i]
    group_wait(RELAY)
    group_wait(ONCE)
    group_wait(TWICE)
    group_wait(THEN)
    once, twice = get(group[ONCE][1]), get(group[TWICE][1]) + get(group[THEN][1])
    once = once[:1] + get(group[RELAY][1]) + once[1:]
    for i in range(2):
        out_cp[0, i] = kept[BASE_P][i] + (last[i] + early[i]) + once[i + 3] + twice[i + 3]
    velocity(
        [kept[BASE_X][i] + added[i] + once[i] + twice[i] for i in range(3)],
        0.5 * COARSE,
        lambda c, i: iv[c, i],
        out_cv,
    )

    for name in SPACE_MESSAGES:
        pl.when(has_right)(lambda name=name: space_copy(name, True).wait_send())
        pl.when(has_left)(lambda name=name: space_copy(name, False).wait_send())
    for name in GROUP_MESSAGES:
        pl.when(sends_on(name))(lambda name=name: group_copy(name).wait_send())


def write_out(*refs):
    store = [pltpu.make_async_copy(refs[i], refs[i + 4], refs[8].at[i]) for i in range(4)]
    for copy in store:
        copy.start()
    for copy in store:
        copy.wait()


def on_device(*args):
    def planes(n):
        return pltpu.VMEM((n, NY, NZ), jnp.float32)

    scratch = []
    for right, left in SPACE_MESSAGES.values():
        scratch += [planes(right), planes(right), planes(left), planes(left)]
    for name, (n, _, _) in GROUP_MESSAGES.items():
        if name == GUESS:
            scratch += [planes(1), pltpu.VMEM((1, 3, 2, NY, NZ), jnp.float32)]
        else:
            scratch += [planes(n), planes(n)]
    scratch += [planes(n) for n in KEPT.values()]
    scratch += [pltpu.VMEM(x.shape, x.dtype) for x in args]
    field, vector = (1, 2, NY, NZ), (1, 3, 2, NY, NZ)
    scratch += [
        pltpu.SemaphoreType.REGULAR((3,)),
        pltpu.SemaphoreType.DMA((len(SPACE_MESSAGES), 4)),
        pltpu.SemaphoreType.DMA((len(GROUP_MESSAGES), 2)),
        pltpu.SemaphoreType.DMA((len(args),)),
    ]
    shapes = [jax.ShapeDtypeStruct(x, jnp.float32) for x in (field, vector, field, vector)]
    results = pl.pallas_call(
        kernel,
        out_shape=[pltpu.VMEM(x.shape, x.dtype) for x in shapes],
        in_specs=[pl.BlockSpec(memory_space=pltpu.HBM)] * 6,
        out_specs=[pl.BlockSpec(memory_space=pltpu.VMEM)] * 4,
        scratch_shapes=scratch,
        compiler_params=pltpu.CompilerParams(
            collective_id=0, has_side_effects=True, vmem_limit_bytes=24 << 20
        ),
        cost_estimate=pl.CostEstimate(
            flops=10_000_000, bytes_accessed=2_000_000, transcendentals=0
        ),
    )(*[pltpu.with_memory_space_constraint(x, pltpu.HBM) for x in args])
    return pl.pallas_call(
        write_out,
        out_shape=shapes,
        in_specs=[pl.BlockSpec(memory_space=pltpu.VMEM)] * 4,
        out_specs=[pl.BlockSpec(memory_space=pltpu.HBM)] * 4,
        scratch_shapes=[pltpu.SemaphoreType.DMA((4,))],
        compiler_params=pltpu.CompilerParams(vmem_limit_bytes=24 << 20),
        cost_estimate=pl.CostEstimate(flops=0, bytes_accessed=1_000_000, transcendentals=0),
    )(*results)


def solution(mesh):
    placed = (
        P(TM, SPACE, None, None),
        P(TM, None, SPACE, None, None),
        P(SPACE, None, None),
        P(None, SPACE, None, None),
        P(SPACE, None, None),
        P(SPACE, None, None),
    )
    return jax.shard_map(
        on_device,
        mesh=mesh,
        in_specs=placed,
        out_specs=(
            P(TM, SPACE, None, None),
            P(TM, None, SPACE, None, None),
            P(TM, SPACE, None, None),
            P(TM, None, SPACE, None, None),
        ),
        check_vma=False,
    )
```

```python
import functools

import jax
import jax.numpy as jnp
from jax import lax
from jax.experimental import pallas as pl
from jax.experimental.pallas import tpu as pltpu
from jax.sharding import PartitionSpec as P

FINE = 0.4 / 4
COARSE = 0.4
NY, NZ = 64, 128
MESH = pl.DeviceIdType.MESH
SPACE, TM = "space", "tm"
(STATIC, SPREAD, INITIAL, FINE1, FINE2, FINE3, LATE, FIRST1, FIRST2, FIRST3) = range(10)
(GUESS, MID, EARLY, SUMS, LAST, RELAY, ONCE, TWICE, THEN) = range(9)
(MASS, STIFF, RATE, BEFORE, TOTAL, FUTURE, START, RELAXED, RATE0, RATE1, BEFORE1, TOTAL1, BASE_P, BASE_X) = range(14)

SPACE_MESSAGES = {
    STATIC: (4, 5),
    SPREAD: (1, 2),
    INITIAL: (3, 4),
    FINE1: (2, 2),
    FINE2: (2, 2),
    FINE3: (2, 2),
    LATE: (2, 2),
    FIRST1: (2, 2),
    FIRST2: (2, 2),
    FIRST3: (1, 1),
}
ONWARD = (FINE2, FINE3, LATE)
GROUP_MESSAGES = {
    GUESS: (6, 1, 0),
    MID: (2, 1, 0),
    EARLY: (3, 1, 0),
    SUMS: (3, 1, 0),
    LAST: (2, 1, 0),
    RELAY: (2, 1, 1),
    ONCE: (3, 2, 0),
    TWICE: (3, 3, 0),
    THEN: (2, 3, 0),
}
KEPT = {
    MASS: 5,
    STIFF: 4,
    RATE: 4,
    BEFORE: 2,
    TOTAL: 4,
    FUTURE: 4,
    START: 3,
    RELAXED: 2,
    RATE0: 4,
    RATE1: 4,
    BEFORE1: 2,
    TOTAL1: 4,
    BASE_P: 2,
    BASE_X: 3,
}


def lower_y(x):
    return pltpu.roll(x, 1, 0)


def upper_y(x):
    return pltpu.roll(x, NY - 1, 0)


def lower_z(x):
    return pltpu.roll(x, 1, 1)


def upper_z(x):
    return pltpu.roll(x, NZ - 1, 1)


def zone_part(x):
    below = lower_z(x)
    s = below + x
    t = 0.5 * (below - x)
    return s, lower_y(s), t + lower_y(t)


def corner_forces(zones):
    parts = [x if isinstance(x, tuple) else zone_part(x) for x in zones]
    forces = []
    for (s0, r0, t0), (s1, r1, t1) in zip(parts[:-1], parts[1:]):
        forces.append((r0 - s1, s0 - r1, t0 + t1))
    return forces


def gather(less, plus, along):
    a = less + upper_y(plus)
    b = along + upper_y(along)
    return (a - b) + upper_z(a + b)


def curve(zones, mass, stiff):
    weighted = [
        (m * a, m * b, m * c) for (a, b, c), m in zip(corner_forces(zones), mass)
    ]
    out = []
    for (a0, b0, c0), (a1, b1, c1), k in zip(weighted[:-1], weighted[1:], stiff):
        out.append(k * gather(b1 - a0, a1 - b0, c0 + c1))
    return out


def spread_up(v):
    return gather(v[0] - v[1], v[0] + v[1], v[2])


def spread_down(v):
    return gather(-v[0] - v[1], v[1] - v[0], v[2])


def kernel(gp_far, gv_far, ip_far, iv_far, k_far, m_far, *rest):
    (out_cp, out_cv, out_rp, out_rv), bufs = rest[:4], list(rest[4:])
    space = {}
    for name in SPACE_MESSAGES:
        space[name] = tuple(bufs.pop(0) for _ in range(4))
    group = {}
    for name in GROUP_MESSAGES:
        group[name] = tuple(bufs.pop(0) for _ in range(2))
    kept = {name: bufs.pop(0) for name in KEPT}
    near = bufs[:6]
    gp, gv, ip, iv, stiffness, inv_mass = near
    ready, space_sems, group_sems, near_sems = bufs[6:]

    s, t = lax.axis_index(SPACE), lax.axis_index(TM)
    n_s, n_t = lax.axis_size(SPACE), lax.axis_size(TM)
    has_left, has_right = s > 0, s < n_s - 1
    goes_on = t + 1 < n_t

    def to_right(name):
        return has_right & goes_on if name in ONWARD else has_right

    def to_left(name):
        return has_left & goes_on if name in ONWARD else has_left

    def space_copy(name, right):
        i = name
        out_right, from_left, out_left, from_right = space[name]
        return pltpu.make_async_remote_copy(
            src_ref=out_right if right else out_left,
            dst_ref=from_left if right else from_right,
            send_sem=space_sems.at[i, 0 if right else 1],
            recv_sem=space_sems.at[i, 2 if right else 3],
            device_id={SPACE: s + 1 if right else s - 1},
            device_id_type=MESH,
        )

    def space_send(name):
        odd = lax.rem(s, 2) == 1
        pl.when(to_right(name) & odd)(lambda: space_copy(name, True).start())
        pl.when(to_left(name))(lambda: space_copy(name, False).start())
        pl.when(to_right(name) & jnp.logical_not(odd))(lambda: space_copy(name, True).start())

    def space_wait(name):
        pl.when(to_left(name))(lambda: space_copy(name, True).wait_recv())
        pl.when(to_right(name))(lambda: space_copy(name, False).wait_recv())

    def group_copy(name):
        i = name
        ahead = GROUP_MESSAGES[name][1]
        return pltpu.make_async_remote_copy(
            src_ref=group[name][0] if name != GUESS else gv,
            dst_ref=group[name][1],
            send_sem=group_sems.at[i, 0],
            recv_sem=group_sems.at[i, 1],
            device_id={TM: t + ahead},
            device_id_type=MESH,
        )

    def sends_on(name):
        _, ahead, first = GROUP_MESSAGES[name]
        return (t >= first) & (t + ahead < n_t)

    def hears(name):
        _, ahead, first = GROUP_MESSAGES[name]
        return t >= ahead + first

    def heard(ahead):
        pl.when(t + ahead < n_t)(lambda: pl.semaphore_wait(ready.at[ahead - 1], 1))

    def group_send(name):
        pl.when(sends_on(name))(lambda: group_copy(name).start())

    def group_wait(name):
        pl.when(hears(name))(lambda: group_copy(name).wait_recv())

    barrier = pltpu.get_barrier_semaphore()

    def tell(where):
        pl.semaphore_signal(barrier, inc=1, device_id=where, device_id_type=MESH)

    pl.when(has_right)(lambda: tell({SPACE: s + 1}))
    pl.when(has_left)(lambda: tell({SPACE: s - 1}))
    for ahead in range(1, 4):
        pl.when(t + ahead < n_t)(lambda ahead=ahead: tell({TM: t + ahead}))

    fetched = {}
    far = (gp_far, gv_far, ip_far, iv_far, k_far, m_far)
    for i in (0, 4, 5, 1, 2, 3):
        fetched[i] = pltpu.make_async_copy(far[i], near[i], near_sems.at[i])
        fetched[i].start()

    def put(ref, planes):
        for i, x in enumerate(planes):
            ref[i] = x

    def get(ref):
        return [ref[i] for i in range(ref.shape[0])]

    nothing = jnp.zeros((NY, NZ), jnp.float32)

    @pl.when(s == 0)
    def _():
        for name in SPACE_MESSAGES:
            ref = space[name][1]
            put(ref, [nothing] * ref.shape[0])

    @pl.when(s == n_s - 1)
    def _():
        for name in SPACE_MESSAGES:
            ref = space[name][3]
            put(ref, [nothing] * ref.shape[0])

    @pl.when(jnp.logical_not(goes_on))
    def _():
        for name in ONWARD:
            put(space[name][1], [nothing] * 2)
            put(space[name][3], [nothing] * 2)

    for name in (RELAY, ONCE, TWICE, THEN):

        @pl.when(jnp.logical_not(hears(name)))
        def _(name=name):
            put(group[name][1], [nothing] * GROUP_MESSAGES[name][0])

    for i in (0, 4, 5):
        fetched[i].wait()
    put(space[STATIC][0], [gp[0, 0], gp[0, 1], stiffness[1], inv_mass[1]])
    put(space[STATIC][2], [gp[0, 0], gp[0, 1], stiffness[0], inv_mass[0], inv_mass[1]])

    fetched[1].wait()
    v0 = [gv[0, i, 0] for i in range(3)]
    v1 = [gv[0, i, 1] for i in range(3)]
    guess_up, guess_d0 = spread_up(v0), spread_up(v1) + spread_down(v0)
    guess_d1 = spread_down(v1)
    put(space[SPREAD][0], [guess_d1])
    put(space[SPREAD][2], [guess_up, guess_d0])

    peers = has_right.astype(jnp.int32) + has_left.astype(jnp.int32) + t
    pl.semaphore_wait(barrier, peers)
    space_send(STATIC)
    space_send(SPREAD)
    for back in range(1, 4):

        @pl.when(t >= back)
        def _(back=back):
            pl.semaphore_signal(
                ready.at[back - 1], inc=1, device_id={TM: t - back}, device_id_type=MESH
            )

    fetched[2].wait()
    fetched[3].wait()
    v0 = [iv[i, 0] for i in range(3)]
    v1 = [iv[i, 1] for i in range(3)]
    first_up, first_d0 = spread_up(v0), spread_up(v1) + spread_down(v0)
    first_d1 = spread_down(v1)
    put(space[INITIAL][0], [ip[0], ip[1], first_d1])
    put(space[INITIAL][2], [ip[0], ip[1], first_up, first_d0])
    space_send(INITIAL)

    def mass():
        return get(kept[MASS])

    def stiff(scale=None):
        return get(kept[STIFF])

    def fine_pair(zones, rate, own=None):
        m, k = mass(), stiff()
        parts = zones[:2] + (own or zones[2:4]) + zones[4:]
        rate = [r - c for r, c in zip(rate, curve(parts, m, k))]
        p1 = [x + r for x, r in zip(zones[1:-1], rate)]
        rate2 = [r - c for r, c in zip(rate[1:3], curve(p1, m[1:4], k[1:3]))]
        p2 = [x + r for x, r in zip(p1[1:3], rate2)]
        return p1, rate, p2, rate2

    def zones_of(name, own):
        left, right = get(space[name][1]), get(space[name][3])
        return left[:2] + own + right[:2]

    def next_rate(zones, before, own):
        return [zones[1] - before[0], own[0], own[1], zones[4] - before[1]]

    own_parts = [zone_part(gp[0, 0]), zone_part(gp[0, 1])]
    space_wait(STATIC)
    left, right = get(space[STATIC][1]), get(space[STATIC][3])
    put(kept[MASS], [left[3], inv_mass[0], inv_mass[1], right[3], right[4]])
    scale = 0.125 * FINE * FINE
    raw = [left[2], stiffness[0], stiffness[1], right[2]]
    put(kept[STIFF], [scale * k for k in raw])
    zones = left[:2] + [gp[0, 0], gp[0, 1]] + right[:2]
    space_wait(SPREAD)
    left, right = get(space[SPREAD][1]), get(space[SPREAD][3])
    spread = [left[0] + guess_up, guess_d0, guess_d1 + right[0], right[1]]
    rate = [(-0.25 * FINE) * k * d for k, d in zip(raw, spread)]
    p1, rate1, p2, rate2 = fine_pair(zones, rate, own_parts)
    put(space[FINE1][0], p2)
    put(space[FINE1][2], p2)
    space_send(FINE1)
    heard(1)
    group_send(GUESS)
    put(kept[RATE], [rate2[0], rate2[0], rate2[1], rate2[1]])
    put(kept[BEFORE], [p1[0], p1[3]])
    put(kept[TOTAL], [x + y for x, y in zip(zones[1:5], p1)])

    space_wait(INITIAL)
    left, right = get(space[INITIAL][1]), get(space[INITIAL][3])
    zones = left[:2] + [ip[0], ip[1]] + right[:2]
    raw = [k * (-0.25 * FINE / scale) for k in stiff()]
    spread = [left[2] + first_up, first_d0, first_d1 + right[2], right[3]]
    rate = [k * d for k, d in zip(raw, spread)]
    put(kept[RATE0], rate)
    p1, rate1, p2, rate2 = fine_pair(zones, rate)
    put(space[FIRST1][0], p2)
    put(space[FIRST1][2], p2)
    space_send(FIRST1)
    put(kept[RATE1], [rate2[0], rate2[0], rate2[1], rate2[1]])
    put(kept[BEFORE1], [p1[0], p1[3]])
    put(kept[TOTAL1], [x + y for x, y in zip(zones[1:5], p1)])

    own_parts = [zone_part(x) for x in get(space[FINE1][0])]
    space_wait(FINE1)
    zones = zones_of(FINE1, get(space[FINE1][0]))
    old = get(kept[RATE])
    rate = next_rate(zones, get(kept[BEFORE]), [old[1], old[2]])
    p1, rate1, p2, rate2 = fine_pair(zones, rate, own_parts)
    put(space[FINE2][0], p2)
    put(space[FINE2][2], p2)
    space_send(FINE2)
    put(kept[RATE], [rate2[0], rate2[0], rate2[1], rate2[1]])
    put(kept[BEFORE], [p1[0], p1[3]])
    total = [x + y + z for x, y, z in zip(get(kept[TOTAL]), zones[1:5], p1)]
    put(kept[TOTAL], total)
    put(kept[START], total[:3])
    put(kept[RELAXED], p2)
    put(group[MID][0], [total[1] + 4.0 * p2[0], total[2] + 4.0 * p2[1]])
    group_send(MID)

    space_wait(FIRST1)
    zones = zones_of(FIRST1, get(space[FIRST1][0]))
    old = get(kept[RATE1])
    rate = next_rate(zones, get(kept[BEFORE1]), [old[1], old[2]])
    p1, rate1, p2, rate2 = fine_pair(zones, rate)
    total1 = [x + y + z for x, y, z in zip(get(kept[TOTAL1]), zones[1:5], p1)]
    put(kept[TOTAL1], [0.25 * x for x in total1])
    moved = [p2[0] + 0.25 * total1[1], p2[1] + 0.25 * total1[2]]
    put(space[FIRST2][0], moved)
    put(space[FIRST2][2], moved)
    space_send(FIRST2)

    @pl.when(t == 0)
    def _():
        put(kept[BASE_P], p2)
        put(kept[BASE_X], [0.25 * x for x in total1[:3]])
        put(group[EARLY][1], [-p2[0], -p2[1], total1[0]])
        put(group[MID][1], total1[1:3])
        put(group[SUMS][1], [nothing] * 3)
        put(group[LAST][1], p2)
        for i in range(3):
            for j in range(2):
                group[GUESS][1][0, i, j] = iv[i, j]

    put(kept[BEFORE1], p2)

    own_parts = [zone_part(x) for x in get(space[FINE2][0])]
    space_wait(FINE2)
    zones = zones_of(FINE2, get(space[FINE2][0]))
    old = get(kept[RATE])
    rate = next_rate(zones, get(kept[BEFORE]), [old[1], old[2]])
    p1, rate1, p2, rate2 = fine_pair(zones, rate, own_parts)
    put(space[FINE3][0], p2)
    put(space[FINE3][2], p2)
    space_send(FINE3)
    ahead = [12.0 * rate[i] - 16.0 * rate1[i] - zones[i + 1] for i in (1, 2)]
    put(group[EARLY][0], ahead + [kept[START][0] + 4.0 * zones[1]])
    group_send(EARLY)
    put(kept[FUTURE], ahead + ahead)
    put(kept[RATE], [rate2[0], rate2[0], rate2[1], rate2[1]])
    put(kept[BEFORE], [p1[0], p1[3]])
    put(kept[TOTAL], [0.25 * (y - 3.0 * x) for x, y in zip(zones[1:5], p1)])

    def coarse_first(zones, value, source, own=None):
        k = [16.0 * x for x in stiff()]
        parts = zones[:2] + (own or zones[2:4]) + zones[4:]
        one = [x - c for x, c in zip(value, curve(parts, mass(), k))]
        if source is not None:
            one = [x + y for x, y in zip(one, source)]
        return one, [x + y for x, y in zip(zones[1:5], one)]

    def coarse_second(one, sums, source):
        k = [16.0 * x for x in stiff()]
        two = [x - c for x, c in zip(one[1:3], curve(sums, mass()[1:4], k[1:3]))]
        if source is not None:
            two = [x + y for x, y in zip(two, source[1:3])]
        return two

    own_parts = [zone_part(x) for x in get(space[FINE3][0])]
    space_wait(FINE3)
    zones = zones_of(FINE3, get(space[FINE3][0]))
    old = get(kept[RATE])
    rate = next_rate(zones, get(kept[BEFORE]), [old[1], old[2]])
    p1, rate1, p2, rate2 = fine_pair(zones, rate, own_parts)
    total = [x + 0.25 * (y + z) for x, y, z in zip(get(kept[TOTAL]), zones[1:5], p1)]
    ahead = get(kept[FUTURE])
    moved = [total[i + 1] + p2[i] + ahead[i] for i in (0, 1)]
    put(space[LATE][0], moved)
    put(space[LATE][2], moved)
    space_send(LATE)
    put(group[SUMS][0], total[:3])
    group_send(SUMS)
    put(group[LAST][0], p2)
    group_send(LAST)
    put(kept[TOTAL], total)
    put(kept[BEFORE], [p2[0] + ahead[0], p2[1] + ahead[1]])

    space_wait(FIRST2)
    zones = zones_of(FIRST2, get(space[FIRST2][0]))
    x0, own = get(kept[TOTAL1]), get(kept[BEFORE1])
    value = [zones[1] - x0[0], own[0], own[1], zones[4] - x0[3]]
    source = [4.0 * x for x in get(kept[RATE0])]
    one, sums = coarse_first(zones, value, source)
    two = coarse_second(one, sums, source)
    third = [sums[1] + two[0], sums[2] + two[1]]
    put(space[FIRST3][0], [third[1]])
    put(space[FIRST3][2], [third[0]])
    space_send(FIRST3)

    @pl.when(t == 1)
    def _():
        put(kept[BASE_P], one[1:3])
        put(kept[BASE_X], zones[1:4])

    @pl.when(t == 2)
    def _():
        put(kept[BASE_P], two)
        put(kept[BASE_X], sums[:3])

    put(kept[BEFORE1], two)
    put(kept[RATE1], third + third)

    own_parts = [zone_part(x) for x in get(space[LATE][0])]
    space_wait(LATE)
    zones = zones_of(LATE, get(space[LATE][0]))
    x0, own = get(kept[TOTAL]), get(kept[BEFORE])
    value = [zones[1] - x0[0], own[0], own[1], zones[4] - x0[3]]
    one, sums = coarse_first(zones, value, None, own_parts)
    put(group[TWICE][0], sums[:3])
    heard(3)
    group_send(TWICE)
    put(group[ONCE][0], [zones[1]] + one[1:3])
    heard(2)
    group_send(ONCE)
    put(group[THEN][0], coarse_second(one, sums, None))
    group_send(THEN)

    group_wait(EARLY)
    group_wait(SUMS)
    group_wait(LAST)
    early, added, last = get(group[EARLY][1]), get(group[SUMS][1]), get(group[LAST][1])
    put(group[RELAY][0], [added[i + 1] + (last[i] + early[i]) for i in (0, 1)])
    group_send(RELAY)

    space_wait(FIRST3)

    @pl.when(t == 3)
    def _():
        left, right = space[FIRST3][1][0], space[FIRST3][3][0]
        own, old = get(kept[RATE1]), get(kept[BEFORE1])
        source = get(kept[RATE0])
        zones = [left, own[0], own[1], right]
        k = [16.0 * x for x in stiff()]
        change = curve(zones, mass()[1:4], k[1:3])
        put(kept[BASE_P], [old[i] + 4.0 * source[i + 1] - change[i] for i in (0, 1)])
        put(kept[BASE_X], [left, own[0], own[1]])

    def velocity(planes, scale, base, out):
        for i, (a, b, c) in enumerate(corner_forces(planes)):
            m = scale * inv_mass[i]
            out[0, 0, i] = base(0, i) + (0.5 * m) * (a + b)
            out[0, 1, i] = base(1, i) + (0.5 * m) * (a - b)
            out[0, 2, i] = base(2, i) + m * c

    group_wait(GUESS)
    group_wait(MID)
    early, added, last = get(group[EARLY][1]), get(group[SUMS][1]), get(group[LAST][1])
    whole = early[2:] + get(group[MID][1])
    start = get(kept[START])
    velocity(
        [whole[i] + 4.0 * added[i] - start[i] for i in range(3)],
        0.5 * FINE,
        lambda c, i: group[GUESS][1][0, c, i] - gv[0, c, i],
        out_rv,
    )
    for i in range(2):
        out_rp[0, i] = last[i] - kept[RELAXED][i]
    group_wait(RELAY)
    group_wait(ONCE)
    group_wait(TWICE)
    group_wait(THEN)
    once, twice = get(group[ONCE][1]), get(group[TWICE][1]) + get(group[THEN][1])
    once = once[:1] + get(group[RELAY][1]) + once[1:]
    for i in range(2):
        out_cp[0, i] = kept[BASE_P][i] + (last[i] + early[i]) + once[i + 3] + twice[i + 3]
    velocity(
        [kept[BASE_X][i] + added[i] + once[i] + twice[i] for i in range(3)],
        0.5 * COARSE,
        lambda c, i: iv[c, i],
        out_cv,
    )

    for name in SPACE_MESSAGES:
        pl.when(to_right(name))(lambda name=name: space_copy(name, True).wait_send())
        pl.when(to_left(name))(lambda name=name: space_copy(name, False).wait_send())
    for name in GROUP_MESSAGES:
        pl.when(sends_on(name))(lambda name=name: group_copy(name).wait_send())


def write_out(*refs):
    store = [pltpu.make_async_copy(refs[i], refs[i + 4], refs[8].at[i]) for i in range(4)]
    for copy in store:
        copy.start()
    for copy in store:
        copy.wait()


def on_device(*args):
    def planes(n):
        return pltpu.VMEM((n, NY, NZ), jnp.float32)

    scratch = []
    for right, left in SPACE_MESSAGES.values():
        scratch += [planes(right), planes(right), planes(left), planes(left)]
    for name, (n, _, _) in GROUP_MESSAGES.items():
        if name == GUESS:
            scratch += [planes(1), pltpu.VMEM((1, 3, 2, NY, NZ), jnp.float32)]
        else:
            scratch += [planes(n), planes(n)]
    scratch += [planes(n) for n in KEPT.values()]
    scratch += [pltpu.VMEM(x.shape, x.dtype) for x in args]
    field, vector = (1, 2, NY, NZ), (1, 3, 2, NY, NZ)
    scratch += [
        pltpu.SemaphoreType.REGULAR((3,)),
        pltpu.SemaphoreType.DMA((len(SPACE_MESSAGES), 4)),
        pltpu.SemaphoreType.DMA((len(GROUP_MESSAGES), 2)),
        pltpu.SemaphoreType.DMA((len(args),)),
    ]
    shapes = [jax.ShapeDtypeStruct(x, jnp.float32) for x in (field, vector, field, vector)]
    results = pl.pallas_call(
        kernel,
        out_shape=[pltpu.VMEM(x.shape, x.dtype) for x in shapes],
        in_specs=[pl.BlockSpec(memory_space=pltpu.HBM)] * 6,
        out_specs=[pl.BlockSpec(memory_space=pltpu.VMEM)] * 4,
        scratch_shapes=scratch,
        compiler_params=pltpu.CompilerParams(
            collective_id=0, has_side_effects=True, vmem_limit_bytes=24 << 20
        ),
        cost_estimate=pl.CostEstimate(
            flops=10_000_000, bytes_accessed=2_000_000, transcendentals=0
        ),
    )(*[pltpu.with_memory_space_constraint(x, pltpu.HBM) for x in args])
    return pl.pallas_call(
        write_out,
        out_shape=shapes,
        in_specs=[pl.BlockSpec(memory_space=pltpu.VMEM)] * 4,
        out_specs=[pl.BlockSpec(memory_space=pltpu.HBM)] * 4,
        scratch_shapes=[pltpu.SemaphoreType.DMA((4,))],
        compiler_params=pltpu.CompilerParams(vmem_limit_bytes=24 << 20),
        cost_estimate=pl.CostEstimate(flops=0, bytes_accessed=1_000_000, transcendentals=0),
    )(*results)


def solution(mesh):
    placed = (
        P(TM, SPACE, None, None),
        P(TM, None, SPACE, None, None),
        P(SPACE, None, None),
        P(None, SPACE, None, None),
        P(SPACE, None, None),
        P(SPACE, None, None),
    )
    return jax.shard_map(
        on_device,
        mesh=mesh,
        in_specs=placed,
        out_specs=(
            P(TM, SPACE, None, None),
            P(TM, None, SPACE, None, None),
            P(TM, SPACE, None, None),
            P(TM, None, SPACE, None, None),
        ),
        check_vma=False,
    )
```

```python
import functools

import jax
import jax.numpy as jnp
from jax import lax
from jax.experimental import pallas as pl
from jax.experimental.pallas import tpu as pltpu
from jax.sharding import PartitionSpec as P

FINE = 0.4 / 4
COARSE = 0.4
NY, NZ = 64, 128
MESH = pl.DeviceIdType.MESH
SPACE, TM = "space", "tm"
(STATIC, SPREAD, INITIAL, FINE1, FINE2, FINE3, LATE, FIRST1, FIRST2, FIRST3) = range(10)
(GUESS, MID, EARLY, SUMS, LAST, RELAY, ONCE, TWICE, THEN) = range(9)
(MASS, STIFF, RATE, BEFORE, TOTAL, FUTURE, START, RELAXED, RATE0, RATE1, BEFORE1, TOTAL1, BASE_P, BASE_X) = range(14)

SPACE_MESSAGES = {
    STATIC: (4, 5),
    SPREAD: (1, 2),
    INITIAL: (3, 4),
    FINE1: (2, 2),
    FINE2: (2, 2),
    FINE3: (2, 2),
    LATE: (2, 2),
    FIRST1: (2, 2),
    FIRST2: (2, 2),
    FIRST3: (1, 1),
}
ONWARD = (FINE2, FINE3, LATE)
GROUP_MESSAGES = {
    GUESS: (6, 1, 0),
    MID: (2, 1, 0),
    EARLY: (3, 1, 0),
    SUMS: (3, 1, 0),
    LAST: (2, 1, 0),
    RELAY: (2, 1, 1),
    ONCE: (3, 2, 0),
    TWICE: (3, 3, 0),
    THEN: (2, 3, 0),
}
KEPT = {
    MASS: 5,
    STIFF: 4,
    RATE: 4,
    BEFORE: 2,
    TOTAL: 4,
    FUTURE: 4,
    START: 3,
    RELAXED: 2,
    RATE0: 4,
    RATE1: 4,
    BEFORE1: 2,
    TOTAL1: 4,
    BASE_P: 2,
    BASE_X: 3,
}


def lower_y(x):
    return pltpu.roll(x, 1, 0)


def upper_y(x):
    return pltpu.roll(x, NY - 1, 0)


def lower_z(x):
    return pltpu.roll(x, 1, 1)


def upper_z(x):
    return pltpu.roll(x, NZ - 1, 1)


def zone_part(x):
    below = lower_z(x)
    s = below + x
    t = 0.5 * (below - x)
    return s, lower_y(s), t + lower_y(t)


def corner_forces(zones):
    parts = [x if isinstance(x, tuple) else zone_part(x) for x in zones]
    forces = []
    for (s0, r0, t0), (s1, r1, t1) in zip(parts[:-1], parts[1:]):
        forces.append((r0 - s1, s0 - r1, t0 + t1))
    return forces


def gather(less, plus, along):
    a = less + upper_y(plus)
    b = along + upper_y(along)
    return (a - b) + upper_z(a + b)


def curve(zones, mass, stiff):
    weighted = [
        (m * a, m * b, m * c) for (a, b, c), m in zip(corner_forces(zones), mass)
    ]
    out = []
    for (a0, b0, c0), (a1, b1, c1), k in zip(weighted[:-1], weighted[1:], stiff):
        out.append(k * gather(b1 - a0, a1 - b0, c0 + c1))
    return out


def spread_up(v):
    return gather(v[0] - v[1], v[0] + v[1], v[2])


def spread_down(v):
    return gather(-v[0] - v[1], v[1] - v[0], v[2])


def kernel(gp_far, gv_far, ip_far, iv_far, k_far, m_far, *rest):
    (out_cp, out_cv, out_rp, out_rv), bufs = rest[:4], list(rest[4:])
    space = {}
    for name in SPACE_MESSAGES:
        space[name] = tuple(bufs.pop(0) for _ in range(4))
    group = {}
    for name in GROUP_MESSAGES:
        group[name] = tuple(bufs.pop(0) for _ in range(2))
    kept = {name: bufs.pop(0) for name in KEPT}
    near = bufs[:6]
    gp, gv, ip, iv, stiffness, inv_mass = near
    ready, space_sems, group_sems, near_sems = bufs[6:]

    s, t = lax.axis_index(SPACE), lax.axis_index(TM)
    n_s, n_t = lax.axis_size(SPACE), lax.axis_size(TM)
    has_left, has_right = s > 0, s < n_s - 1
    goes_on = t + 1 < n_t

    def to_right(name):
        return has_right & goes_on if name in ONWARD else has_right

    def to_left(name):
        return has_left & goes_on if name in ONWARD else has_left

    def space_copy(name, right):
        i = name
        out_right, from_left, out_left, from_right = space[name]
        return pltpu.make_async_remote_copy(
            src_ref=out_right if right else out_left,
            dst_ref=from_left if right else from_right,
            send_sem=space_sems.at[i, 0 if right else 1],
            recv_sem=space_sems.at[i, 2 if right else 3],
            device_id={SPACE: s + 1 if right else s - 1},
            device_id_type=MESH,
        )

    def space_send(name):
        odd = lax.rem(s, 2) == 1
        pl.when(to_right(name) & odd)(lambda: space_copy(name, True).start())
        pl.when(to_left(name))(lambda: space_copy(name, False).start())
        pl.when(to_right(name) & jnp.logical_not(odd))(lambda: space_copy(name, True).start())

    def space_wait(name):
        pl.when(to_left(name))(lambda: space_copy(name, True).wait_recv())
        pl.when(to_right(name))(lambda: space_copy(name, False).wait_recv())

    def group_copy(name):
        i = name
        ahead = GROUP_MESSAGES[name][1]
        return pltpu.make_async_remote_copy(
            src_ref=group[name][0] if name != GUESS else gv,
            dst_ref=group[name][1],
            send_sem=group_sems.at[i, 0],
            recv_sem=group_sems.at[i, 1],
            device_id={TM: t + ahead},
            device_id_type=MESH,
        )

    def sends_on(name):
        _, ahead, first = GROUP_MESSAGES[name]
        return (t >= first) & (t + ahead < n_t)

    def hears(name):
        _, ahead, first = GROUP_MESSAGES[name]
        return t >= ahead + first

    def heard(ahead):
        pl.when(t + ahead < n_t)(lambda: pl.semaphore_wait(ready.at[ahead - 1], 1))

    def group_send(name):
        pl.when(sends_on(name))(lambda: group_copy(name).start())

    def group_wait(name):
        pl.when(hears(name))(lambda: group_copy(name).wait_recv())

    barrier = pltpu.get_barrier_semaphore()

    def tell(where):
        pl.semaphore_signal(barrier, inc=1, device_id=where, device_id_type=MESH)

    pl.when(has_right)(lambda: tell({SPACE: s + 1}))
    pl.when(has_left)(lambda: tell({SPACE: s - 1}))
    for ahead in range(1, 4):
        pl.when(t + ahead < n_t)(lambda ahead=ahead: tell({TM: t + ahead}))

    fetched = {}
    far = (gp_far, gv_far, ip_far, iv_far, k_far, m_far)
    for i in (0, 4, 5, 1, 2, 3):
        fetched[i] = pltpu.make_async_copy(far[i], near[i], near_sems.at[i])
        fetched[i].start()

    def put(ref, planes):
        for i, x in enumerate(planes):
            ref[i] = x

    def get(ref):
        return [ref[i] for i in range(ref.shape[0])]

    nothing = jnp.zeros((NY, NZ), jnp.float32)

    @pl.when(s == 0)
    def _():
        for name in SPACE_MESSAGES:
            ref = space[name][1]
            put(ref, [nothing] * ref.shape[0])

    @pl.when(s == n_s - 1)
    def _():
        for name in SPACE_MESSAGES:
            ref = space[name][3]
            put(ref, [nothing] * ref.shape[0])

    @pl.when(jnp.logical_not(goes_on))
    def _():
        for name in ONWARD:
            put(space[name][1], [nothing] * 2)
            put(space[name][3], [nothing] * 2)

    for name in (RELAY, ONCE, TWICE, THEN):

        @pl.when(jnp.logical_not(hears(name)))
        def _(name=name):
            put(group[name][1], [nothing] * GROUP_MESSAGES[name][0])

    for i in (0, 4, 5):
        fetched[i].wait()
    put(space[STATIC][0], [gp[0, 0], gp[0, 1], stiffness[1], inv_mass[1]])
    put(space[STATIC][2], [gp[0, 0], gp[0, 1], stiffness[0], inv_mass[0], inv_mass[1]])

    fetched[1].wait()
    v0 = [gv[0, i, 0] for i in range(3)]
    v1 = [gv[0, i, 1] for i in range(3)]
    guess_up, guess_d0 = spread_up(v0), spread_up(v1) + spread_down(v0)
    guess_d1 = spread_down(v1)
    put(space[SPREAD][0], [guess_d1])
    put(space[SPREAD][2], [guess_up, guess_d0])

    peers = has_right.astype(jnp.int32) + has_left.astype(jnp.int32) + t
    pl.semaphore_wait(barrier, peers)
    space_send(STATIC)
    space_send(SPREAD)
    for back in range(1, 4):

        @pl.when(t >= back)
        def _(back=back):
            pl.semaphore_signal(
                ready.at[back - 1], inc=1, device_id={TM: t - back}, device_id_type=MESH
            )

    fetched[2].wait()
    fetched[3].wait()
    v0 = [iv[i, 0] for i in range(3)]
    v1 = [iv[i, 1] for i in range(3)]
    first_up, first_d0 = spread_up(v0), spread_up(v1) + spread_down(v0)
    first_d1 = spread_down(v1)
    put(space[INITIAL][0], [ip[0], ip[1], first_d1])
    put(space[INITIAL][2], [ip[0], ip[1], first_up, first_d0])
    space_send(INITIAL)

    def mass():
        return get(kept[MASS])

    def stiff(scale=None):
        return get(kept[STIFF])

    def fine_pair(zones, rate, own=None):
        m, k = mass(), stiff()
        parts = zones[:2] + (own or zones[2:4]) + zones[4:]
        rate = [r - c for r, c in zip(rate, curve(parts, m, k))]
        p1 = [x + r for x, r in zip(zones[1:-1], rate)]
        rate2 = [r - c for r, c in zip(rate[1:3], curve(p1, m[1:4], k[1:3]))]
        p2 = [x + r for x, r in zip(p1[1:3], rate2)]
        return p1, rate, p2, rate2

    def zones_of(name, own):
        left, right = get(space[name][1]), get(space[name][3])
        return left[:2] + own + right[:2]

    def next_rate(zones, before, own):
        return [zones[1] - before[0], own[0], own[1], zones[4] - before[1]]

    own_parts = [zone_part(gp[0, 0]), zone_part(gp[0, 1])]
    space_wait(STATIC)
    left, right = get(space[STATIC][1]), get(space[STATIC][3])
    put(kept[MASS], [left[3], inv_mass[0], inv_mass[1], right[3], right[4]])
    scale = 0.125 * FINE * FINE
    raw = [left[2], stiffness[0], stiffness[1], right[2]]
    put(kept[STIFF], [scale * k for k in raw])
    zones = left[:2] + [gp[0, 0], gp[0, 1]] + right[:2]
    space_wait(SPREAD)
    heard(1)
    group_send(GUESS)
    left, right = get(space[SPREAD][1]), get(space[SPREAD][3])
    spread = [left[0] + guess_up, guess_d0, guess_d1 + right[0], right[1]]
    rate = [(-0.25 * FINE) * k * d for k, d in zip(raw, spread)]
    p1, rate1, p2, rate2 = fine_pair(zones, rate, own_parts)
    put(space[FINE1][0], p2)
    put(space[FINE1][2], p2)
    space_send(FINE1)
    put(kept[RATE], [rate2[0], rate2[0], rate2[1], rate2[1]])
    put(kept[BEFORE], [p1[0], p1[3]])
    put(kept[TOTAL], [x + y for x, y in zip(zones[1:5], p1)])

    space_wait(INITIAL)
    left, right = get(space[INITIAL][1]), get(space[INITIAL][3])
    zones = left[:2] + [ip[0], ip[1]] + right[:2]
    raw = [k * (-0.25 * FINE / scale) for k in stiff()]
    spread = [left[2] + first_up, first_d0, first_d1 + right[2], right[3]]
    rate = [k * d for k, d in zip(raw, spread)]
    put(kept[RATE0], rate)
    p1, rate1, p2, rate2 = fine_pair(zones, rate)
    put(space[FIRST1][0], p2)
    put(space[FIRST1][2], p2)
    space_send(FIRST1)
    put(kept[RATE1], [rate2[0], rate2[0], rate2[1], rate2[1]])
    put(kept[BEFORE1], [p1[0], p1[3]])
    put(kept[TOTAL1], [x + y for x, y in zip(zones[1:5], p1)])

    own_parts = [zone_part(x) for x in get(space[FINE1][0])]
    space_wait(FINE1)
    zones = zones_of(FINE1, get(space[FINE1][0]))
    old = get(kept[RATE])
    rate = next_rate(zones, get(kept[BEFORE]), [old[1], old[2]])
    p1, rate1, p2, rate2 = fine_pair(zones, rate, own_parts)
    put(space[FINE2][0], p2)
    put(space[FINE2][2], p2)
    space_send(FINE2)
    put(kept[RATE], [rate2[0], rate2[0], rate2[1], rate2[1]])
    put(kept[BEFORE], [p1[0], p1[3]])
    total = [x + y + z for x, y, z in zip(get(kept[TOTAL]), zones[1:5], p1)]
    put(kept[TOTAL], total)
    put(kept[START], total[:3])
    put(kept[RELAXED], p2)
    put(group[MID][0], [total[1] + 4.0 * p2[0], total[2] + 4.0 * p2[1]])
    group_send(MID)

    space_wait(FIRST1)
    zones = zones_of(FIRST1, get(space[FIRST1][0]))
    old = get(kept[RATE1])
    rate = next_rate(zones, get(kept[BEFORE1]), [old[1], old[2]])
    p1, rate1, p2, rate2 = fine_pair(zones, rate)
    total1 = [x + y + z for x, y, z in zip(get(kept[TOTAL1]), zones[1:5], p1)]
    put(kept[TOTAL1], [0.25 * x for x in total1])
    moved = [p2[0] + 0.25 * total1[1], p2[1] + 0.25 * total1[2]]
    put(space[FIRST2][0], moved)
    put(space[FIRST2][2], moved)
    space_send(FIRST2)

    @pl.when(t == 0)
    def _():
        put(kept[BASE_P], p2)
        put(kept[BASE_X], [0.25 * x for x in total1[:3]])
        put(group[EARLY][1], [-p2[0], -p2[1], total1[0]])
        put(group[MID][1], total1[1:3])
        put(group[SUMS][1], [nothing] * 3)
        put(group[LAST][1], p2)
        for i in range(3):
            for j in range(2):
                group[GUESS][1][0, i, j] = iv[i, j]

    put(kept[BEFORE1], p2)

    own_parts = [zone_part(x) for x in get(space[FINE2][0])]
    space_wait(FINE2)
    zones = zones_of(FINE2, get(space[FINE2][0]))
    old = get(kept[RATE])
    rate = next_rate(zones, get(kept[BEFORE]), [old[1], old[2]])
    p1, rate1, p2, rate2 = fine_pair(zones, rate, own_parts)
    put(space[FINE3][0], p2)
    put(space[FINE3][2], p2)
    space_send(FINE3)
    ahead = [12.0 * rate[i] - 16.0 * rate1[i] - zones[i + 1] for i in (1, 2)]
    put(group[EARLY][0], ahead + [kept[START][0] + 4.0 * zones[1]])
    group_send(EARLY)
    put(kept[FUTURE], ahead + ahead)
    put(kept[RATE], [rate2[0], rate2[0], rate2[1], rate2[1]])
    put(kept[BEFORE], [p1[0], p1[3]])
    put(kept[TOTAL], [0.25 * (y - 3.0 * x) for x, y in zip(zones[1:5], p1)])

    def coarse_first(zones, value, source, own=None):
        k = [16.0 * x for x in stiff()]
        parts = zones[:2] + (own or zones[2:4]) + zones[4:]
        one = [x - c for x, c in zip(value, curve(parts, mass(), k))]
        if source is not None:
            one = [x + y for x, y in zip(one, source)]
        return one, [x + y for x, y in zip(zones[1:5], one)]

    def coarse_second(one, sums, source):
        k = [16.0 * x for x in stiff()]
        two = [x - c for x, c in zip(one[1:3], curve(sums, mass()[1:4], k[1:3]))]
        if source is not None:
            two = [x + y for x, y in zip(two, source[1:3])]
        return two

    own_parts = [zone_part(x) for x in get(space[FINE3][0])]
    space_wait(FINE3)
    zones = zones_of(FINE3, get(space[FINE3][0]))
    old = get(kept[RATE])
    rate = next_rate(zones, get(kept[BEFORE]), [old[1], old[2]])
    p1, rate1, p2, rate2 = fine_pair(zones, rate, own_parts)
    total = [x + 0.25 * (y + z) for x, y, z in zip(get(kept[TOTAL]), zones[1:5], p1)]
    ahead = get(kept[FUTURE])
    moved = [total[i + 1] + p2[i] + ahead[i] for i in (0, 1)]
    put(space[LATE][0], moved)
    put(space[LATE][2], moved)
    space_send(LATE)
    put(group[SUMS][0], total[:3])
    group_send(SUMS)
    put(group[LAST][0], p2)
    group_send(LAST)
    put(kept[TOTAL], total)
    put(kept[BEFORE], [p2[0] + ahead[0], p2[1] + ahead[1]])

    space_wait(FIRST2)
    zones = zones_of(FIRST2, get(space[FIRST2][0]))
    x0, own = get(kept[TOTAL1]), get(kept[BEFORE1])
    value = [zones[1] - x0[0], own[0], own[1], zones[4] - x0[3]]
    source = [4.0 * x for x in get(kept[RATE0])]
    one, sums = coarse_first(zones, value, source)
    two = coarse_second(one, sums, source)
    third = [sums[1] + two[0], sums[2] + two[1]]
    put(space[FIRST3][0], [third[1]])
    put(space[FIRST3][2], [third[0]])
    space_send(FIRST3)

    @pl.when(t == 1)
    def _():
        put(kept[BASE_P], one[1:3])
        put(kept[BASE_X], zones[1:4])

    @pl.when(t == 2)
    def _():
        put(kept[BASE_P], two)
        put(kept[BASE_X], sums[:3])

    put(kept[BEFORE1], two)
    put(kept[RATE1], third + third)

    own_parts = [zone_part(x) for x in get(space[LATE][0])]
    space_wait(LATE)
    zones = zones_of(LATE, get(space[LATE][0]))
    x0, own = get(kept[TOTAL]), get(kept[BEFORE])
    value = [zones[1] - x0[0], own[0], own[1], zones[4] - x0[3]]
    one, sums = coarse_first(zones, value, None, own_parts)
    put(group[TWICE][0], sums[:3])
    heard(3)
    group_send(TWICE)
    put(group[ONCE][0], [zones[1]] + one[1:3])
    heard(2)
    group_send(ONCE)
    put(group[THEN][0], coarse_second(one, sums, None))
    group_send(THEN)

    group_wait(EARLY)
    group_wait(SUMS)
    group_wait(LAST)
    early, added, last = get(group[EARLY][1]), get(group[SUMS][1]), get(group[LAST][1])
    put(group[RELAY][0], [added[i + 1] + (last[i] + early[i]) for i in (0, 1)])
    group_send(RELAY)

    space_wait(FIRST3)

    @pl.when(t == 3)
    def _():
        left, right = space[FIRST3][1][0], space[FIRST3][3][0]
        own, old = get(kept[RATE1]), get(kept[BEFORE1])
        source = get(kept[RATE0])
        zones = [left, own[0], own[1], right]
        k = [16.0 * x for x in stiff()]
        change = curve(zones, mass()[1:4], k[1:3])
        put(kept[BASE_P], [old[i] + 4.0 * source[i + 1] - change[i] for i in (0, 1)])
        put(kept[BASE_X], [left, own[0], own[1]])

    def velocity(planes, scale, base, out):
        for i, (a, b, c) in enumerate(corner_forces(planes)):
            m = scale * inv_mass[i]
            out[0, 0, i] = base(0, i) + (0.5 * m) * (a + b)
            out[0, 1, i] = base(1, i) + (0.5 * m) * (a - b)
            out[0, 2, i] = base(2, i) + m * c

    group_wait(GUESS)
    group_wait(MID)
    early, added, last = get(group[EARLY][1]), get(group[SUMS][1]), get(group[LAST][1])
    whole = early[2:] + get(group[MID][1])
    start = get(kept[START])
    velocity(
        [whole[i] + 4.0 * added[i] - start[i] for i in range(3)],
        0.5 * FINE,
        lambda c, i: group[GUESS][1][0, c, i] - gv[0, c, i],
        out_rv,
    )
    for i in range(2):
        out_rp[0, i] = last[i] - kept[RELAXED][i]
    group_wait(RELAY)
    group_wait(ONCE)
    group_wait(TWICE)
    group_wait(THEN)
    once, twice = get(group[ONCE][1]), get(group[TWICE][1]) + get(group[THEN][1])
    once = once[:1] + get(group[RELAY][1]) + once[1:]
    for i in range(2):
        out_cp[0, i] = kept[BASE_P][i] + (last[i] + early[i]) + once[i + 3] + twice[i + 3]
    velocity(
        [kept[BASE_X][i] + added[i] + once[i] + twice[i] for i in range(3)],
        0.5 * COARSE,
        lambda c, i: iv[c, i],
        out_cv,
    )

    for name in SPACE_MESSAGES:
        pl.when(to_right(name))(lambda name=name: space_copy(name, True).wait_send())
        pl.when(to_left(name))(lambda name=name: space_copy(name, False).wait_send())
    for name in GROUP_MESSAGES:
        pl.when(sends_on(name))(lambda name=name: group_copy(name).wait_send())


def write_out(*refs):
    store = [pltpu.make_async_copy(refs[i], refs[i + 4], refs[8].at[i]) for i in range(4)]
    for copy in store:
        copy.start()
    for copy in store:
        copy.wait()


def on_device(*args):
    def planes(n):
        return pltpu.VMEM((n, NY, NZ), jnp.float32)

    scratch = []
    for right, left in SPACE_MESSAGES.values():
        scratch += [planes(right), planes(right), planes(left), planes(left)]
    for name, (n, _, _) in GROUP_MESSAGES.items():
        if name == GUESS:
            scratch += [planes(1), pltpu.VMEM((1, 3, 2, NY, NZ), jnp.float32)]
        else:
            scratch += [planes(n), planes(n)]
    scratch += [planes(n) for n in KEPT.values()]
    scratch += [pltpu.VMEM(x.shape, x.dtype) for x in args]
    field, vector = (1, 2, NY, NZ), (1, 3, 2, NY, NZ)
    scratch += [
        pltpu.SemaphoreType.REGULAR((3,)),
        pltpu.SemaphoreType.DMA((len(SPACE_MESSAGES), 4)),
        pltpu.SemaphoreType.DMA((len(GROUP_MESSAGES), 2)),
        pltpu.SemaphoreType.DMA((len(args),)),
    ]
    shapes = [jax.ShapeDtypeStruct(x, jnp.float32) for x in (field, vector, field, vector)]
    results = pl.pallas_call(
        kernel,
        out_shape=[pltpu.VMEM(x.shape, x.dtype) for x in shapes],
        in_specs=[pl.BlockSpec(memory_space=pltpu.HBM)] * 6,
        out_specs=[pl.BlockSpec(memory_space=pltpu.VMEM)] * 4,
        scratch_shapes=scratch,
        compiler_params=pltpu.CompilerParams(
            collective_id=0, has_side_effects=True, vmem_limit_bytes=24 << 20
        ),
        cost_estimate=pl.CostEstimate(
            flops=10_000_000, bytes_accessed=2_000_000, transcendentals=0
        ),
    )(*[pltpu.with_memory_space_constraint(x, pltpu.HBM) for x in args])
    return pl.pallas_call(
        write_out,
        out_shape=shapes,
        in_specs=[pl.BlockSpec(memory_space=pltpu.VMEM)] * 4,
        out_specs=[pl.BlockSpec(memory_space=pltpu.HBM)] * 4,
        scratch_shapes=[pltpu.SemaphoreType.DMA((4,))],
        compiler_params=pltpu.CompilerParams(vmem_limit_bytes=24 << 20),
        cost_estimate=pl.CostEstimate(flops=0, bytes_accessed=1_000_000, transcendentals=0),
    )(*results)


def solution(mesh):
    placed = (
        P(TM, SPACE, None, None),
        P(TM, None, SPACE, None, None),
        P(SPACE, None, None),
        P(None, SPACE, None, None),
        P(SPACE, None, None),
        P(SPACE, None, None),
    )
    return jax.shard_map(
        on_device,
        mesh=mesh,
        in_specs=placed,
        out_specs=(
            P(TM, SPACE, None, None),
            P(TM, None, SPACE, None, None),
            P(TM, SPACE, None, None),
            P(TM, None, SPACE, None, None),
        ),
        check_vma=False,
    )
```
